32 devices in a mesh: lon: 8 (over z, x), lat: 4 (over y, core).
Axes of the slice: x: 2, y: 2, z: 4, core: 2. Of those that a mesh axis runs over, the one named last changes fastest.
Arguments:
- pressure: float32 [4, 960, 2048], P(None, 'lat', 'lon'), may hold values from -6 to 6
- wind_east: float32 [4, 960, 2048], P(None, 'lat', 'lon'), may hold values from -6 to 6
- wind_north: float32 [4, 960, 2048], P(None, 'lat', 'lon'), may hold values from -6 to 6
- forcing: float32 [4, 960, 2048], P(None, 'lat', 'lon'), may hold values from -6 to 6
- coef_lon: float32 [4, 960, 2048], P(None, 'lat', 'lon'), may hold values from 0.2 to 2
- coef_lat: float32 [4, 960, 2048], P(None, 'lat', 'lon'), may hold values from 0.2 to 2
- coef_vert: float32 [4, 960, 2048], P(None, 'lat', 'lon'), may hold values from 0.2 to 2
- diag_coef: float32 [4, 960, 2048], P(None, 'lat', 'lon'), may hold values from 0.5 to 2
Outputs:
- new_pressure: float32 [4, 960, 2048], P(None, 'lat', 'lon')
- residual: float32 [4, 960, 2048], P(None, 'lat', 'lon')
The draws below stay inside these ranges and needn't reach their ends.
All inputs are finite; a program needn't handle non-finite values.
Results may differ from the reference program's by a relative error of at most 0.00002.
Values sent between devices are 32-bit elements; how exact they have to be, the bound alone decides.
A program may use at most 128 MiB of HBM per device.

```python
import math
import jax
import jax.numpy as jnp

LEV = 4
NLAT = 960
NLON = 2048


def block_scale(key, dims, split, least, largest):
    factor_of = 1.0
    for axis_at, blocks in split:
        steps = jax.random.uniform(jax.random.fold_in(jax.random.fold_in(key, 6), axis_at), (blocks,), jnp.float32, least / len(split), largest / len(split))
        factor_of = factor_of * jnp.repeat(jnp.exp(steps), dims[axis_at] // blocks).reshape((-1,) + (1,) * (len(dims) - 1 - axis_at))
    return factor_of


def bell_draw(stream_key, shape, scale, limit, shards=(), kind=jnp.bfloat16):
    entries = scale * jax.random.normal(stream_key, shape, jnp.float32)
    if shards:
        entries = entries * block_scale(stream_key, shape, shards, -0.22, 0.18)
    return jnp.clip(entries, -limit, limit).astype(kind)


def setup_inputs(seed: int = 0) -> dict:
    key_list = jax.random.split(jax.random.key(seed), 9)
    pressure = bell_draw(key_list[0], (LEV, NLAT, NLON), 1.0, 6.0, ((1, 4), (2, 8)), jnp.float32)
    wind_east = bell_draw(key_list[1], (LEV, NLAT, NLON), 1.0, 6.0, ((1, 4), (2, 8)), jnp.float32)
    wind_north = bell_draw(key_list[2], (LEV, NLAT, NLON), 1.0, 6.0, ((1, 4), (2, 8)), jnp.float32)
    forcing = bell_draw(key_list[3], (LEV, NLAT, NLON), 1.0, 6.0, ((1, 4), (2, 8)), jnp.float32)
    coef_lon = jnp.clip(jnp.exp(math.log(2.0) - 2.3025851 * jax.random.uniform(key_list[4], (LEV, NLAT, NLON), jnp.float32) ** block_scale(key_list[4], (LEV, NLAT, NLON), ((1, 4), (2, 8)), -0.2, 0.2)), 0.2, 2.0)
    coef_lat = jnp.clip(jnp.exp(math.log(2.0) - 2.3025851 * jax.random.uniform(key_list[5], (LEV, NLAT, NLON), jnp.float32) ** block_scale(key_list[5], (LEV, NLAT, NLON), ((1, 4), (2, 8)), -0.2, 0.2)), 0.2, 2.0)
    coef_vert = jnp.clip(jnp.exp(math.log(2.0) - 2.3025851 * jax.random.uniform(key_list[6], (LEV, NLAT, NLON), jnp.float32) ** block_scale(key_list[6], (LEV, NLAT, NLON), ((1, 4), (2, 8)), -0.2, 0.2)), 0.2, 2.0)
    diag_coef = jnp.clip(jnp.exp(math.log(2.0) - 1.3862944 * jax.random.uniform(key_list[7], (LEV, NLAT, NLON), jnp.float32) ** block_scale(key_list[7], (LEV, NLAT, NLON), ((1, 4), (2, 8)), -0.2, 0.2)), 0.5, 2.0)
    return {"pressure": pressure, "wind_east": wind_east, "wind_north": wind_north, "forcing": forcing, "coef_lon": coef_lon, "coef_lat": coef_lat, "coef_vert": coef_vert, "diag_coef": diag_coef}


def face_cosines(start_row, face_count, lat_total):
    positions = (start_row + jnp.arange(face_count, dtype=jnp.int32)).astype(jnp.float32)
    return jnp.cos(positions * (math.pi / lat_total) - math.pi / 2)


def divergence(east_ext, north_ext, face_cos):
    cos_low = face_cos[:-1][None, :, None]
    cos_high = face_cos[1:][None, :, None]
    middle = north_ext[:, 1:-1, 1:-1]
    zonal = 0.5 * (east_ext[:, 1:-1, 2:] - east_ext[:, 1:-1, :-2])
    merid = 0.5 * (cos_high * (middle + north_ext[:, 2:, 1:-1]) - cos_low * (north_ext[:, :-2, 1:-1] + middle))
    return zonal + merid


def helmholtz(field_ext, lon_ext, lat_ext, vert_coef, diag_coef, face_cos):
    centre = field_ext[:, 1:-1, 1:-1]
    lon_mid = lon_ext[:, 1:-1, 1:-1]
    west_weight = 0.5 * (lon_mid + lon_ext[:, 1:-1, :-2])
    east_weight = 0.5 * (lon_mid + lon_ext[:, 1:-1, 2:])
    metric = 0.5 * (1.0 + jnp.abs(face_cos))
    lat_mid = lat_ext[:, 1:-1, 1:-1]
    south_weight = metric[:-1][None, :, None] * (0.5 * (lat_mid + lat_ext[:, :-2, 1:-1]))
    north_weight = metric[1:][None, :, None] * (0.5 * (lat_mid + lat_ext[:, 2:, 1:-1]))
    zero_level = jnp.zeros_like(centre[:1])
    upper_weight = jnp.concatenate((vert_coef[1:], jnp.zeros_like(vert_coef[:1])), 0)
    below = jnp.concatenate((zero_level, centre[:-1]), 0)
    above = jnp.concatenate((centre[1:], zero_level), 0)
    diag_total = diag_coef + west_weight + east_weight + south_weight + north_weight + vert_coef + upper_weight
    coupled = (west_weight * field_ext[:, 1:-1, :-2] + east_weight * field_ext[:, 1:-1, 2:]
               + south_weight * field_ext[:, :-2, 1:-1] + north_weight * field_ext[:, 2:, 1:-1]
               + vert_coef * below + upper_weight * above)
    return diag_total * centre - coupled, diag_total


def extend_field(field, rim_width):
    south_rim = jnp.roll(jnp.flip(field[:, :rim_width], 1), NLON // 2, 2)
    north_rim = jnp.roll(jnp.flip(field[:, -rim_width:], 1), NLON // 2, 2)
    tall = jnp.concatenate((south_rim, field, north_rim), 1)
    return jnp.concatenate((tall[:, :, -rim_width:], tall, tall[:, :, :rim_width]), 2)


def reference(pressure, wind_east, wind_north, forcing, coef_lon, coef_lat, coef_vert, diag_coef):
    face_cos = face_cosines(0, NLAT + 1, NLAT)
    lon_ext = extend_field(coef_lon, 1)
    lat_ext = extend_field(coef_lat, 1)
    rhs_field = forcing - divergence(extend_field(wind_east, 1), extend_field(wind_north, 1), face_cos)
    applied, diag_total = helmholtz(extend_field(pressure, 1), lon_ext, lat_ext, coef_vert, diag_coef, face_cos)
    new_pressure = pressure + (rhs_field - applied) / diag_total
    applied_new, unused = helmholtz(extend_field(new_pressure, 1), lon_ext, lat_ext, coef_vert, diag_coef, face_cos)
    return new_pressure, rhs_field - applied_new
```

```python
import functools
import math

import jax
import jax.numpy as jnp
from jax import lax
from jax.experimental import pallas as pl
from jax.experimental.pallas import tpu as pltpu
from jax.sharding import PartitionSpec as P

LANES = 128
SUB = 8
MESH = pl.DeviceIdType.MESH


def kernel(
    lon_n, lat_n, lat_total,
    p_in, we_in, wn_in, f_in, cl_in, ct_in, cv_in, dg_in,
    np_out, res_out,
    pb, web, wnb, fb, clb, ctb, cvb, dgb,
    npb, rhsb, wwb, web2, swb, cosb,
    pk, hc, col_send, col_recv, row_send, row_recv,
    col2_send, col2_recv, row2_send, row2_recv,
    in_sem, out_sem, send_sem, recv_sem,
):
    levels, tiles, rows = web.shape[0], web.shape[1], web.shape[2]
    blocks = pk.shape[0] // LANES
    chunks = rows // SUB
    lon = lax.axis_index("lon")
    lat = lax.axis_index("lat")
    east = (lat_id(lon + 1, lon_n), lat)
    west = (lat_id(lon + lon_n - 1, lon_n), lat)
    across = lat_id(lon + lon_n // 2, lon_n)
    at_south = jnp.int32(lat == 0)
    at_north = jnp.int32(lat == lat_n - 1)
    south = (lon + at_south * (across - lon), lat - 1 + at_south)
    north = (lon + at_north * (across - lon), lat + 1 - at_north)
    partners = (west, east, south, north)

    loads = []
    for a, (src, dst, pad) in enumerate((
        (p_in, pb, SUB), (we_in, web, 0), (cl_in, clb, 0), (wn_in, wnb, SUB),
        (ct_in, ctb, SUB), (f_in, fb, 0), (cv_in, cvb, 0), (dg_in, dgb, 0),
    )):
        group = []
        for t in range(tiles):
            copy = pltpu.make_async_copy(
                src.at[:, :, pl.ds(t * LANES, LANES)],
                dst.at[:, t, pl.ds(pad, rows), :],
                in_sem.at[a, t],
            )
            copy.start()
            group.append(copy)
        loads.append(group)

    barrier = pltpu.get_barrier_semaphore()
    for lo, la in partners:
        pl.semaphore_signal(barrier, inc=1, device_id=(lo, la), device_id_type=MESH)

    lane = lax.broadcasted_iota(jnp.int32, (SUB, LANES), 1)
    lane4 = lax.broadcasted_iota(jnp.int32, (levels, tiles, SUB, LANES), 3)

    def cos_step(i, _):
        r = pl.multiple_of(i * SUB, SUB)
        face = lat * rows + r + lax.broadcasted_iota(jnp.int32, (SUB, LANES), 0)
        angle = face.astype(jnp.float32) * (math.pi / lat_total) - math.pi / 2
        cosb[pl.ds(r, SUB), :] = jnp.cos(angle)
        return 0

    lax.fori_loop(0, chunks + 1, cos_step, 0)

    def wait_load(*which):
        for a in which:
            for copy in loads[a]:
                copy.wait()

    def pack_columns(fields, pads, width):
        def step(i, _):
            r = pl.multiple_of(i * SUB, SUB)
            acc = jnp.zeros((SUB, LANES), jnp.float32)
            for f, (ref, pad) in enumerate(zip(fields, pads)):
                for k in range(levels):
                    n = f * levels + k
                    last = ref[k, tiles - 1, pl.ds(r + pad, SUB), :]
                    acc = jnp.where(lane == n, pltpu.roll(last, n + 1, 1), acc)
                    first = ref[k, 0, pl.ds(r + pad, SUB), :]
                    acc = jnp.where(lane == width + n, pltpu.roll(first, width + n, 1), acc)
            pk[pl.ds(r, SUB), :] = acc
            return 0

        lax.fori_loop(0, chunks, step, 0)

    def columns_to_rows(dst, width):
        for u in range(blocks):
            turned = pk[pl.ds(u * LANES, LANES), :].T
            dst[0, u] = turned[:width]
            dst[1, u] = turned[width:2 * width]

    def rows_to_columns(src, width):
        for u in range(blocks):
            both = jnp.concatenate(
                (src[0, u], src[1, u], jnp.zeros((LANES - 2 * width, LANES), jnp.float32)), 0
            )
            hc[pl.ds(u * LANES, LANES), :] = both.T

    def send(n, src, dst, target, slot, phase):
        copy = pltpu.make_async_remote_copy(
            src_ref=src, dst_ref=dst,
            send_sem=send_sem.at[phase, n], recv_sem=recv_sem.at[phase, slot],
            device_id=target, device_id_type=MESH,
        )
        copy.start()
        return copy

    def wait_recv(dst, slot, phase):
        pltpu.make_async_remote_copy(
            src_ref=dst, dst_ref=dst,
            send_sem=send_sem.at[phase, slot], recv_sem=recv_sem.at[phase, slot],
            device_id=east, device_id_type=MESH,
        ).wait_recv()

    south_slot = 1 - at_south
    north_slot = at_north

    def send_all(cs, cr, rs, rr, phase):
        return (
            send(0, cs.at[0], cr.at[0], east, 0, phase),
            send(1, cs.at[1], cr.at[1], west, 1, phase),
            send(2, rs.at[0], rr.at[south_slot], south, 2 + south_slot, phase),
            send(3, rs.at[1], rr.at[north_slot], north, 2 + north_slot, phase),
        )

    def pack_rows(fields, dst):
        for f, ref in enumerate(fields):
            for k in range(levels):
                n = f * levels + k
                for t in range(tiles):
                    dst[0, t, n:n + 1, :] = ref[k, t, SUB:SUB + 1, :]
                    dst[1, t, n:n + 1, :] = ref[k, t, SUB + rows - 1:SUB + rows, :]

    def unpack_rows(src, fields):
        for f, ref in enumerate(fields):
            for k in range(levels):
                n = f * levels + k
                for t in range(tiles):
                    ref[k, t, SUB - 1:SUB, :] = src[0, t, n:n + 1, :]
                    ref[k, t, SUB + rows:SUB + rows + 1, :] = src[1, t, n:n + 1, :]

    if blocks * LANES > rows:
        pk[pl.ds(rows, blocks * LANES - rows), :] = jnp.zeros(
            (blocks * LANES - rows, LANES), jnp.float32
        )
    wide = col_send.shape[2]
    narrow = col2_send.shape[2]
    row_send[...] = jnp.zeros(row_send.shape, jnp.float32)
    row2_send[...] = jnp.zeros(row2_send.shape, jnp.float32)

    wait_load(0, 1, 2)
    pack_columns((pb, web, clb), (SUB, 0, 0), wide)
    columns_to_rows(col_send, wide)
    wait_load(3, 4)
    pack_rows((pb, wnb, ctb), row_send)
    pl.semaphore_wait(barrier, len(partners))
    sends = send_all(col_send, col_recv, row_send, row_recv, 0)

    wait_load(5, 6, 7)
    for slot in (2, 3):
        wait_recv(row_recv.at[slot - 2], slot, 0)
    unpack_rows(row_recv, (pb, wnb, ctb))
    for slot in (0, 1):
        wait_recv(col_recv.at[slot], slot, 0)
    rows_to_columns(col_recv, wide)

    def halo(r, first, target):
        edge = hc[pl.ds(r, SUB), :]
        return jnp.stack(
            [pltpu.roll(edge, (target - first - k) % LANES, 1) for k in range(levels)]
        )[:, None]

    def shift(x, rim, west_side):
        if west_side:
            turned = pltpu.roll(x, 1, 3)
            beside = jnp.concatenate((rim, turned[:, :-1]), 1) if tiles > 1 else rim
            return jnp.where(lane4 == 0, beside, turned)
        turned = pltpu.roll(x, LANES - 1, 3)
        beside = jnp.concatenate((turned[:, 1:], rim), 1) if tiles > 1 else rim
        return jnp.where(lane4 == LANES - 1, beside, turned)

    def vertical(p, v):
        lower = jnp.concatenate((jnp.zeros_like(p[:1]), p[:-1]), 0)
        flux = v * (p - lower)
        return flux - jnp.concatenate((flux[1:], jnp.zeros_like(p[:1])), 0)

    def first_pass(i, _):
        r = pl.multiple_of(i * SUB, SUB)
        here = pl.ds(r, SUB)
        mid, low, high = pl.ds(r + SUB, SUB), pl.ds(r + SUB - 1, SUB), pl.ds(r + SUB + 1, SUB)
        c_low = cosb[here, :]
        c_high = cosb[pl.ds(r + 1, SUB), :]
        m_low = 0.25 * (1.0 + jnp.abs(c_low))
        m_high = 0.25 * (1.0 + jnp.abs(c_high))
        we = web[:, :, here, :]
        zonal = shift(we, halo(r, wide + levels, LANES - 1), False) - shift(
            we, halo(r, levels, 0), True
        )
        wn = wnb[:, :, mid, :]
        merid = c_high * (wn + wnb[:, :, high, :]) - c_low * (wnb[:, :, low, :] + wn)
        rhs = fb[:, :, here, :] - 0.5 * (zonal + merid)
        rhsb[:, :, here, :] = rhs
        cl = clb[:, :, here, :]
        w_west = 0.5 * (cl + shift(cl, halo(r, 2 * levels, 0), True))
        w_east = 0.5 * (cl + shift(cl, halo(r, wide + 2 * levels, LANES - 1), False))
        wwb[:, :, here, :] = w_west
        web2[:, :, here, :] = w_east
        ct = ctb[:, :, mid, :]
        w_south = m_low * (ct + ctb[:, :, low, :])
        w_north = m_high * (ct + ctb[:, :, high, :])
        swb[:, :, here, :] = w_south
        swb[:, :, pl.ds(r + 1, SUB), :] = w_north
        v = cvb[:, :, here, :]
        dg = dgb[:, :, here, :]
        upper = jnp.concatenate((v[1:], jnp.zeros_like(v[:1])), 0)
        total = dg + w_west + w_east + w_south + w_north + v + upper
        p = pb[:, :, mid, :]
        applied = dg * p + vertical(p, v)
        applied += w_west * (p - shift(p, halo(r, 0, 0), True))
        applied += w_east * (p - shift(p, halo(r, wide, LANES - 1), False))
        applied += w_south * (p - pb[:, :, low, :])
        applied += w_north * (p - pb[:, :, high, :])
        npb[:, :, mid, :] = p + (rhs - applied) / total
        return 0

    lax.fori_loop(0, chunks, first_pass, 0)

    pack_columns((npb,), (SUB,), narrow)
    columns_to_rows(col2_send, narrow)
    pack_rows((npb,), row2_send)
    sends += send_all(col2_send, col2_recv, row2_send, row2_recv, 1)

    stores = []
    for t in range(tiles):
        copy = pltpu.make_async_copy(
            npb.at[:, t, pl.ds(SUB, rows), :],
            np_out.at[:, :, pl.ds(t * LANES, LANES)],
            out_sem.at[0, t],
        )
        copy.start()
        stores.append(copy)

    for slot in (2, 3):
        wait_recv(row2_recv.at[slot - 2], slot, 1)
    unpack_rows(row2_recv, (npb,))
    for slot in (0, 1):
        wait_recv(col2_recv.at[slot], slot, 1)
    rows_to_columns(col2_recv, narrow)

    def second_pass(i, _):
        r = pl.multiple_of(i * SUB, SUB)
        here = pl.ds(r, SUB)
        mid, low, high = pl.ds(r + SUB, SUB), pl.ds(r + SUB - 1, SUB), pl.ds(r + SUB + 1, SUB)
        p = npb[:, :, mid, :]
        applied = dgb[:, :, here, :] * p + vertical(p, cvb[:, :, here, :])
        applied += wwb[:, :, here, :] * (p - shift(p, halo(r, 0, 0), True))
        applied += web2[:, :, here, :] * (p - shift(p, halo(r, narrow, LANES - 1), False))
        applied += swb[:, :, here, :] * (p - npb[:, :, low, :])
        applied += swb[:, :, pl.ds(r + 1, SUB), :] * (p - npb[:, :, high, :])
        rhsb[:, :, here, :] = rhsb[:, :, here, :] - applied
        return 0

    lax.fori_loop(0, chunks, second_pass, 0)

    for t in range(tiles):
        copy = pltpu.make_async_copy(
            rhsb.at[:, t],
            res_out.at[:, :, pl.ds(t * LANES, LANES)],
            out_sem.at[1, t],
        )
        copy.start()
        stores.append(copy)
    for copy in sends:
        copy.wait_send()
    for copy in stores:
        copy.wait()


def lat_id(index, count):
    return lax.rem(index, count)


def per_device(lon_n, lat_n, *fields):
    levels, rows, width = fields[0].shape
    tiles = width // LANES
    blocks = -(-rows // LANES)
    f32 = jnp.float32
    plain = pltpu.VMEM((levels, tiles, rows, LANES), f32)
    padded = pltpu.VMEM((levels, tiles, rows + 2 * SUB, LANES), f32)
    face = pltpu.VMEM((levels, tiles, rows + SUB, LANES), f32)
    wide = -(-3 * levels // SUB) * SUB
    narrow = -(-levels // SUB) * SUB
    cols = lambda n: pltpu.VMEM((2, blocks, n, LANES), f32)
    edge = lambda n: pltpu.VMEM((2, tiles, n, LANES), f32)
    shape = jax.ShapeDtypeStruct((levels, rows, width), f32)
    any_spec = pl.BlockSpec(memory_space=pl.ANY)
    return pl.pallas_call(
        functools.partial(kernel, lon_n, lat_n, rows * lat_n),
        out_shape=(shape, shape),
        in_specs=[any_spec] * 8,
        out_specs=(any_spec, any_spec),
        scratch_shapes=[
            padded, plain, padded, plain, plain, padded, plain, plain,
            padded, plain, plain, plain, face, pltpu.VMEM((rows + 2 * SUB, LANES), f32),
            pltpu.VMEM((blocks * LANES, LANES), f32), pltpu.VMEM((blocks * LANES, LANES), f32),
            cols(wide), cols(wide), edge(wide), edge(wide),
            cols(narrow), cols(narrow), edge(narrow), edge(narrow),
            pltpu.SemaphoreType.DMA((8, tiles)),
            pltpu.SemaphoreType.DMA((2, tiles)),
            pltpu.SemaphoreType.DMA((2, 4)),
            pltpu.SemaphoreType.DMA((2, 4)),
        ],
        compiler_params=pltpu.CompilerParams(
            collective_id=0, has_side_effects=True, vmem_limit_bytes=48 * 1024 * 1024
        ),
    )(*fields)


def solution(mesh):
    spec = P(None, "lat", "lon")
    return jax.shard_map(
        functools.partial(per_device, mesh.shape["lon"], mesh.shape["lat"]),
        mesh=mesh, in_specs=(spec,) * 8, out_specs=(spec, spec), check_vma=False,
    )
```

```python
import functools
import math

import jax
import jax.numpy as jnp
from jax import lax
from jax.experimental import pallas as pl
from jax.experimental.pallas import tpu as pltpu
from jax.sharding import PartitionSpec as P

LANES = 128
SUB = 8
MESH = pl.DeviceIdType.MESH


def kernel(
    lon_n, lat_n, lat_total,
    p_in, we_in, wn_in, f_in, cl_in, ct_in, cv_in, dg_in,
    np_out, res_out,
    pb, web, wnb, fb, clb, ctb, cvb, dgb,
    npb, rhsb, rhs2b, appb, totb, accb, resb, wwb, ewb, swb, nwb, cosb,
    pk, hc, col_send, col_recv, row_send, row_recv,
    col2_send, col2_recv, row2_send, row2_recv,
    in_sem, out_sem, send_sem, recv_sem,
):
    levels, tiles, rows = web.shape[0], web.shape[1], web.shape[2]
    blocks = pk.shape[0] // LANES
    chunks = rows // SUB
    lon = lax.axis_index("lon")
    lat = lax.axis_index("lat")
    east = (lat_id(lon + 1, lon_n), lat)
    west = (lat_id(lon + lon_n - 1, lon_n), lat)
    across = lat_id(lon + lon_n // 2, lon_n)
    at_south = jnp.int32(lat == 0)
    at_north = jnp.int32(lat == lat_n - 1)
    south = (lon + at_south * (across - lon), lat - 1 + at_south)
    north = (lon + at_north * (across - lon), lat + 1 - at_north)
    partners = (west, east, south, north)

    loads = []
    for a, (src, dst, pad) in enumerate((
        (p_in, pb, SUB), (we_in, web, 0), (cl_in, clb, 0), (wn_in, wnb, SUB),
        (ct_in, ctb, SUB), (f_in, fb, 0), (cv_in, cvb, 0), (dg_in, dgb, 0),
    )):
        group = []
        for t in range(tiles):
            copy = pltpu.make_async_copy(
                src.at[:, :, pl.ds(t * LANES, LANES)],
                dst.at[:, t, pl.ds(pad, rows), :],
                in_sem.at[a, t],
            )
            copy.start()
            group.append(copy)
        loads.append(group)

    barrier = pltpu.get_barrier_semaphore()
    for lo, la in partners:
        pl.semaphore_signal(barrier, inc=1, device_id=(lo, la), device_id_type=MESH)

    lane = lax.broadcasted_iota(jnp.int32, (SUB, LANES), 1)
    lane4 = lax.broadcasted_iota(jnp.int32, (levels, tiles, SUB, LANES), 3)

    face = lat * rows + lax.broadcasted_iota(jnp.int32, cosb.shape, 0)
    cosb[...] = jnp.cos(face.astype(jnp.float32) * (math.pi / lat_total) - math.pi / 2)

    def wait_load(*which):
        for a in which:
            for copy in loads[a]:
                copy.wait()

    def loop(first, last, step):
        size = max(n for n in range(1, 6) if (last - first) % n == 0)
        lax.fori_loop(first, last, step, 0, unroll=size)

    def packed(fields, width):
        acc = jnp.zeros((SUB, LANES), jnp.float32)
        for f, field in enumerate(fields):
            for k in range(levels):
                n = f * levels + k
                acc = jnp.where(lane == n, pltpu.roll(field[k, tiles - 1], n + 1, 1), acc)
                acc = jnp.where(lane == width + n, pltpu.roll(field[k, 0], width + n, 1), acc)
        return acc

    def pack_first(i, _):
        r = pl.multiple_of(i * SUB, SUB)
        here = pl.ds(r, SUB)
        pk[here, :] = packed(
            [pb[:, :, pl.ds(r + SUB, SUB), :], web[:, :, here, :], clb[:, :, here, :]], wide
        )
        return 0

    def columns_to_rows(dst, width):
        for u in range(blocks):
            turned = pk[pl.ds(u * LANES, LANES), :].T
            dst[0, u] = turned[:width]
            dst[1, u] = turned[width:2 * width]

    def rows_to_columns(src, width):
        for u in range(blocks):
            both = jnp.concatenate(
                (src[0, u], src[1, u], jnp.zeros((LANES - 2 * width, LANES), jnp.float32)), 0
            )
            hc[pl.ds(u * LANES, LANES), :] = both.T

    def send(n, src, dst, target, slot, phase):
        copy = pltpu.make_async_remote_copy(
            src_ref=src, dst_ref=dst,
            send_sem=send_sem.at[phase, n], recv_sem=recv_sem.at[phase, slot],
            device_id=target, device_id_type=MESH,
        )
        copy.start()
        return copy

    def wait_recv(dst, slot, phase):
        pltpu.make_async_remote_copy(
            src_ref=dst, dst_ref=dst,
            send_sem=send_sem.at[phase, slot], recv_sem=recv_sem.at[phase, slot],
            device_id=east, device_id_type=MESH,
        ).wait_recv()

    south_slot = 1 - at_south
    north_slot = at_north

    def send_all(cs, cr, rs, rr, phase):
        return (
            send(0, cs.at[0], cr.at[0], east, 0, phase),
            send(1, cs.at[1], cr.at[1], west, 1, phase),
            send(2, rs.at[0], rr.at[south_slot], south, 2 + south_slot, phase),
            send(3, rs.at[1], rr.at[north_slot], north, 2 + north_slot, phase),
        )

    def pack_rows(fields, dst):
        for f, ref in enumerate(fields):
            for k in range(levels):
                n = f * levels + k
                for t in range(tiles):
                    dst[0, t, n:n + 1, :] = ref[k, t, SUB:SUB + 1, :]
                    dst[1, t, n:n + 1, :] = ref[k, t, SUB + rows - 1:SUB + rows, :]

    def unpack_rows(src, fields):
        for f, ref in enumerate(fields):
            for k in range(levels):
                n = f * levels + k
                for t in range(tiles):
                    ref[k, t, SUB - 1:SUB, :] = src[0, t, n:n + 1, :]
                    ref[k, t, SUB + rows:SUB + rows + 1, :] = src[1, t, n:n + 1, :]

    if blocks * LANES > rows:
        pk[pl.ds(rows, blocks * LANES - rows), :] = jnp.zeros(
            (blocks * LANES - rows, LANES), jnp.float32
        )
    wide = col_send.shape[2]
    narrow = col2_send.shape[2]
    row_send[...] = jnp.zeros(row_send.shape, jnp.float32)
    row2_send[...] = jnp.zeros(row2_send.shape, jnp.float32)

    wait_load(0, 1, 2)
    loop(0, chunks, pack_first)
    columns_to_rows(col_send, wide)
    wait_load(3, 4)
    pack_rows((pb, wnb, ctb), row_send)
    pl.semaphore_wait(barrier, len(partners))
    sends = send_all(col_send, col_recv, row_send, row_recv, 0)

    wait_load(5, 6, 7)

    def halo(r, first, target):
        edge = hc[pl.ds(r, SUB), :]
        return jnp.stack(
            [pltpu.roll(edge, (target - first - k) % LANES, 1) for k in range(levels)]
        )[:, None]

    def shift(x, rim, west_side):
        if west_side:
            turned = pltpu.roll(x, 1, 3)
            beside = jnp.concatenate((rim, turned[:, :-1]), 1) if tiles > 1 else rim
            return jnp.where(lane4 == 0, beside, turned)
        turned = pltpu.roll(x, LANES - 1, 3)
        beside = jnp.concatenate((turned[:, 1:], rim), 1) if tiles > 1 else rim
        return jnp.where(lane4 == LANES - 1, beside, turned)

    def vertical(p, v):
        lower = jnp.concatenate((jnp.zeros_like(p[:1]), p[:-1]), 0)
        flux = v * (p - lower)
        return flux - jnp.concatenate((flux[1:], jnp.zeros_like(p[:1])), 0)

    def slices(i):
        r = pl.multiple_of(i * SUB, SUB)
        return r, pl.ds(r, SUB), pl.ds(r + SUB, SUB), pl.ds(r + SUB - 1, SUB), pl.ds(r + SUB + 1, SUB)

    def first_inner(i, _):
        r, here, mid, low, high = slices(i)
        c_low = cosb[here, :]
        c_high = cosb[pl.ds(r + 1, SUB), :]
        m_low = 0.25 * (1.0 + jnp.abs(c_low))
        m_high = 0.25 * (1.0 + jnp.abs(c_high))
        wn = wnb[:, :, mid, :]
        merid = c_high * (wn + wnb[:, :, high, :]) - c_low * (wnb[:, :, low, :] + wn)
        rhsb[:, :, here, :] = fb[:, :, here, :] - 0.5 * merid
        ct = ctb[:, :, mid, :]
        w_south = m_low * (ct + ctb[:, :, low, :])
        w_north = m_high * (ct + ctb[:, :, high, :])
        swb[:, :, here, :] = w_south
        nwb[:, :, here, :] = w_north
        v = cvb[:, :, here, :]
        dg = dgb[:, :, here, :]
        upper = jnp.concatenate((v[1:], jnp.zeros_like(v[:1])), 0)
        totb[:, :, here, :] = dg + w_south + w_north + v + upper
        p = pb[:, :, mid, :]
        applied = dg * p + vertical(p, v)
        applied += w_south * (p - pb[:, :, low, :])
        appb[:, :, here, :] = applied + w_north * (p - pb[:, :, high, :])
        return 0

    def first_outer(i, _):
        r, here, mid, low, high = slices(i)
        we = web[:, :, here, :]
        zonal = shift(we, halo(r, wide + levels, LANES - 1), False) - shift(
            we, halo(r, levels, 0), True
        )
        rhs = rhsb[:, :, here, :] - 0.5 * zonal
        rhs2b[:, :, here, :] = rhs
        cl = clb[:, :, here, :]
        w_west = 0.5 * (cl + shift(cl, halo(r, 2 * levels, 0), True))
        w_east = 0.5 * (cl + shift(cl, halo(r, wide + 2 * levels, LANES - 1), False))
        wwb[:, :, here, :] = w_west
        ewb[:, :, here, :] = w_east
        total = totb[:, :, here, :] + w_west + w_east
        p = pb[:, :, mid, :]
        applied = appb[:, :, here, :]
        applied += w_west * (p - shift(p, halo(r, 0, 0), True))
        applied += w_east * (p - shift(p, halo(r, wide, LANES - 1), False))
        fresh = p + (rhs - applied) / total
        npb[:, :, mid, :] = fresh
        pk[here, :] = packed([fresh], narrow)
        return 0

    def second_inner(i, _):
        r, here, mid, low, high = slices(i)
        p = npb[:, :, mid, :]
        applied = dgb[:, :, here, :] * p + vertical(p, cvb[:, :, here, :])
        applied += swb[:, :, here, :] * (p - npb[:, :, low, :])
        applied += nwb[:, :, here, :] * (p - npb[:, :, high, :])
        accb[:, :, here, :] = rhs2b[:, :, here, :] - applied
        return 0

    def second_outer(i, _):
        r, here, mid, low, high = slices(i)
        p = npb[:, :, mid, :]
        acc = accb[:, :, here, :]
        acc -= wwb[:, :, here, :] * (p - shift(p, halo(r, 0, 0), True))
        acc -= ewb[:, :, here, :] * (p - shift(p, halo(r, narrow, LANES - 1), False))
        resb[:, :, here, :] = acc
        return 0

    def inner_rows(step, src, fields, phase):
        loop(1, chunks - 1, step)
        for slot in (2, 3):
            wait_recv(src.at[slot - 2], slot, phase)
        unpack_rows(src, fields)
        step(0, 0)
        step(chunks - 1, 0)

    inner_rows(first_inner, row_recv, (pb, wnb, ctb), 0)
    for slot in (0, 1):
        wait_recv(col_recv.at[slot], slot, 0)
    rows_to_columns(col_recv, wide)
    loop(0, chunks, first_outer)

    columns_to_rows(col2_send, narrow)
    pack_rows((npb,), row2_send)
    sends += send_all(col2_send, col2_recv, row2_send, row2_recv, 1)

    stores = []

    def store(n, src, dst):
        for t in range(tiles):
            copy = pltpu.make_async_copy(
                src(t), dst.at[:, :, pl.ds(t * LANES, LANES)], out_sem.at[n, t]
            )
            copy.start()
            stores.append(copy)

    store(0, lambda t: npb.at[:, t, pl.ds(SUB, rows), :], np_out)
    inner_rows(second_inner, row2_recv, (npb,), 1)
    for slot in (0, 1):
        wait_recv(col2_recv.at[slot], slot, 1)
    rows_to_columns(col2_recv, narrow)
    loop(0, chunks, second_outer)
    store(1, lambda t: resb.at[:, t], res_out)
    for copy in sends:
        copy.wait_send()
    for copy in stores:
        copy.wait()


def lat_id(index, count):
    return lax.rem(index, count)


def per_device(lon_n, lat_n, *fields):
    levels, rows, width = fields[0].shape
    tiles = width // LANES
    blocks = -(-rows // LANES)
    f32 = jnp.float32
    plain = pltpu.VMEM((levels, tiles, rows, LANES), f32)
    padded = pltpu.VMEM((levels, tiles, rows + 2 * SUB, LANES), f32)
    wide = -(-3 * levels // SUB) * SUB
    narrow = -(-levels // SUB) * SUB
    cols = lambda n: pltpu.VMEM((2, blocks, n, LANES), f32)
    edge = lambda n: pltpu.VMEM((2, tiles, n, LANES), f32)
    shape = jax.ShapeDtypeStruct((levels, rows, width), f32)
    any_spec = pl.BlockSpec(memory_space=pl.ANY)
    return pl.pallas_call(
        functools.partial(kernel, lon_n, lat_n, rows * lat_n),
        out_shape=(shape, shape),
        in_specs=[any_spec] * 8,
        out_specs=(any_spec, any_spec),
        scratch_shapes=[
            padded, plain, padded, plain, plain, padded, plain, plain,
            padded] + [plain] * 10 + [pltpu.VMEM((rows + SUB, LANES), f32),
            pltpu.VMEM((blocks * LANES, LANES), f32), pltpu.VMEM((blocks * LANES, LANES), f32),
            cols(wide), cols(wide), edge(wide), edge(wide),
            cols(narrow), cols(narrow), edge(narrow), edge(narrow),
            pltpu.SemaphoreType.DMA((8, tiles)),
            pltpu.SemaphoreType.DMA((2, tiles)),
            pltpu.SemaphoreType.DMA((2, 4)),
            pltpu.SemaphoreType.DMA((2, 4)),
        ],
        compiler_params=pltpu.CompilerParams(
            collective_id=0, has_side_effects=True, vmem_limit_bytes=48 * 1024 * 1024
        ),
    )(*(pltpu.with_memory_space_constraint(x, pltpu.HBM) for x in fields))


def solution(mesh):
    spec = P(None, "lat", "lon")
    return jax.shard_map(
        functools.partial(per_device, mesh.shape["lon"], mesh.shape["lat"]),
        mesh=mesh, in_specs=(spec,) * 8, out_specs=(spec, spec), check_vma=False,
    )
```

```python
import functools
import math

import jax
import jax.numpy as jnp
from jax import lax
from jax.experimental import pallas as pl
from jax.experimental.pallas import tpu as pltpu
from jax.sharding import PartitionSpec as P

LANES = 128
SUB = 8
MESH = pl.DeviceIdType.MESH


def loop(first, last, step):
    size = max(n for n in range(1, 6) if (last - first) % n == 0)
    lax.fori_loop(first, last, step, 0, unroll=size)


def slices(i):
    r = pl.multiple_of(i * SUB, SUB)
    return r, pl.ds(r, SUB), pl.ds(r + SUB, SUB), pl.ds(r + SUB - 1, SUB), pl.ds(r + SUB + 1, SUB)


def halo(hc, levels, r, first, target):
    edge = hc[pl.ds(r, SUB), :]
    return jnp.stack(
        [pltpu.roll(edge, (target - first - k) % LANES, 1) for k in range(levels)]
    )[:, None]


def shift(x, rim, west_side):
    tiles = x.shape[1]
    lane4 = lax.broadcasted_iota(jnp.int32, x.shape, 3)
    if west_side:
        turned = pltpu.roll(x, 1, 3)
        beside = jnp.concatenate((rim, turned[:, :-1]), 1) if tiles > 1 else rim
        return jnp.where(lane4 == 0, beside, turned)
    turned = pltpu.roll(x, LANES - 1, 3)
    beside = jnp.concatenate((turned[:, 1:], rim), 1) if tiles > 1 else rim
    return jnp.where(lane4 == LANES - 1, beside, turned)


def vertical(p, v):
    lower = jnp.concatenate((jnp.zeros_like(p[:1]), p[:-1]), 0)
    flux = v * (p - lower)
    return flux - jnp.concatenate((flux[1:], jnp.zeros_like(p[:1])), 0)


def finish(narrow, npb, accb, wwb, ewb, hc, np_out, res_out, resb, sem):
    levels, tiles, rows = accb.shape[0], accb.shape[1], accb.shape[2]
    chunks = rows // SUB
    parts = max(n for n in range(1, 4) if chunks % n == 0)
    span = rows // parts
    copies = []

    def store(n, part, src, pad, dst):
        for t in range(tiles):
            copy = pltpu.make_async_copy(
                src.at[:, t, pl.ds(part * span + pad, span), :],
                dst.at[:, pl.ds(part * span, span), pl.ds(t * LANES, LANES)],
                sem.at[n, part, t],
            )
            copy.start()
            copies.append(copy)

    def step(i, _):
        r, here, mid, low, high = slices(i)
        p = npb[:, :, mid, :]
        acc = accb[:, :, here, :]
        acc -= wwb[:, :, here, :] * (p - shift(p, halo(hc, levels, r, 0, 0), True))
        acc -= ewb[:, :, here, :] * (
            p - shift(p, halo(hc, levels, r, narrow, LANES - 1), False)
        )
        resb[:, :, here, :] = acc
        return 0

    for part in range(parts):
        store(0, part, npb, SUB, np_out)
    for part in range(parts):
        loop(part * (chunks // parts), (part + 1) * (chunks // parts), step)
        store(1, part, resb, 0, res_out)
    for copy in copies:
        copy.wait()


def kernel(
    lon_n, lat_n, lat_total,
    p_in, we_in, wn_in, f_in, cl_in, ct_in, cv_in, dg_in,
    npb, accb, wwb, ewb, hc,
    pb, web, wnb, fb, clb, ctb, cvb, dgb,
    rhsb, rhs2b, appb, totb, swb, nwb, cosb,
    pk, col_send, col_recv, row_send, row_recv,
    col2_send, col2_recv, row2_send, row2_recv,
    in_sem, send_sem, recv_sem,
):
    levels, tiles, rows = web.shape[0], web.shape[1], web.shape[2]
    blocks = pk.shape[0] // LANES
    chunks = rows // SUB
    lon = lax.axis_index("lon")
    lat = lax.axis_index("lat")
    east = (lat_id(lon + 1, lon_n), lat)
    west = (lat_id(lon + lon_n - 1, lon_n), lat)
    across = lat_id(lon + lon_n // 2, lon_n)
    at_south = jnp.int32(lat == 0)
    at_north = jnp.int32(lat == lat_n - 1)
    south = (lon + at_south * (across - lon), lat - 1 + at_south)
    north = (lon + at_north * (across - lon), lat + 1 - at_north)
    partners = (west, east, south, north)

    loads = []
    for a, (src, dst, pad) in enumerate((
        (p_in, pb, SUB), (we_in, web, 0), (cl_in, clb, 0), (wn_in, wnb, SUB),
        (ct_in, ctb, SUB), (f_in, fb, 0), (cv_in, cvb, 0), (dg_in, dgb, 0),
    )):
        group = []
        for t in range(tiles):
            copy = pltpu.make_async_copy(
                src.at[:, :, pl.ds(t * LANES, LANES)],
                dst.at[:, t, pl.ds(pad, rows), :],
                in_sem.at[a, t],
            )
            group.append(copy)
        loads.append(group)

    def start_load(*which):
        for a in which:
            for copy in loads[a]:
                copy.start()

    start_load(0, 1, 2, 3, 4)

    barrier = pltpu.get_barrier_semaphore()
    for lo, la in partners:
        pl.semaphore_signal(barrier, inc=1, device_id=(lo, la), device_id_type=MESH)

    lane = lax.broadcasted_iota(jnp.int32, (SUB, LANES), 1)

    face = lat * rows + lax.broadcasted_iota(jnp.int32, cosb.shape, 0)
    cosb[...] = jnp.cos(face.astype(jnp.float32) * (math.pi / lat_total) - math.pi / 2)

    def wait_load(*which):
        for a in which:
            for copy in loads[a]:
                copy.wait()

    def packed(fields, width):
        acc = jnp.zeros((SUB, LANES), jnp.float32)
        for f, field in enumerate(fields):
            for k in range(levels):
                n = f * levels + k
                acc = jnp.where(lane == n, pltpu.roll(field[k, tiles - 1], n + 1, 1), acc)
                acc = jnp.where(lane == width + n, pltpu.roll(field[k, 0], width + n, 1), acc)
        return acc

    def pack_first(i, _):
        r = pl.multiple_of(i * SUB, SUB)
        here = pl.ds(r, SUB)
        pk[here, :] = packed(
            [pb[:, :, pl.ds(r + SUB, SUB), :], web[:, :, here, :], clb[:, :, here, :]], wide
        )
        return 0

    def columns_to_rows(dst, width):
        for u in range(blocks):
            turned = pk[pl.ds(u * LANES, LANES), :].T
            dst[0, u] = turned[:width]
            dst[1, u] = turned[width:2 * width]

    def rows_to_columns(src, width):
        for u in range(blocks):
            both = jnp.concatenate(
                (src[0, u], src[1, u], jnp.zeros((LANES - 2 * width, LANES), jnp.float32)), 0
            )
            hc[pl.ds(u * LANES, LANES), :] = both.T

    def send(n, src, dst, target, slot, phase):
        copy = pltpu.make_async_remote_copy(
            src_ref=src, dst_ref=dst,
            send_sem=send_sem.at[phase, n], recv_sem=recv_sem.at[phase, slot],
            device_id=target, device_id_type=MESH,
        )
        copy.start()
        return copy

    def wait_recv(dst, slot, phase):
        pltpu.make_async_remote_copy(
            src_ref=dst, dst_ref=dst,
            send_sem=send_sem.at[phase, slot], recv_sem=recv_sem.at[phase, slot],
            device_id=east, device_id_type=MESH,
        ).wait_recv()

    south_slot = 1 - at_south
    north_slot = at_north

    def send_all(cs, cr, rs, rr, phase):
        return (
            send(0, cs.at[0], cr.at[0], east, 0, phase),
            send(1, cs.at[1], cr.at[1], west, 1, phase),
            send(2, rs.at[0], rr.at[south_slot], south, 2 + south_slot, phase),
            send(3, rs.at[1], rr.at[north_slot], north, 2 + north_slot, phase),
        )

    def pack_rows(fields, dst):
        for f, ref in enumerate(fields):
            for k in range(levels):
                n = f * levels + k
                for t in range(tiles):
                    dst[0, t, n:n + 1, :] = ref[k, t, SUB:SUB + 1, :]
                    dst[1, t, n:n + 1, :] = ref[k, t, SUB + rows - 1:SUB + rows, :]

    def unpack_rows(src, fields):
        for f, ref in enumerate(fields):
            for k in range(levels):
                n = f * levels + k
                for t in range(tiles):
                    ref[k, t, SUB - 1:SUB, :] = src[0, t, n:n + 1, :]
                    ref[k, t, SUB + rows:SUB + rows + 1, :] = src[1, t, n:n + 1, :]

    if blocks * LANES > rows:
        pk[pl.ds(rows, blocks * LANES - rows), :] = jnp.zeros(
            (blocks * LANES - rows, LANES), jnp.float32
        )
    wide = col_send.shape[2]
    narrow = col2_send.shape[2]
    row_send[...] = jnp.zeros(row_send.shape, jnp.float32)
    row2_send[...] = jnp.zeros(row2_send.shape, jnp.float32)

    wait_load(0, 1, 2)
    start_load(5, 6, 7)
    loop(0, chunks, pack_first)
    columns_to_rows(col_send, wide)
    wait_load(3, 4)
    pack_rows((pb, wnb, ctb), row_send)
    pl.semaphore_wait(barrier, len(partners))
    sends = send_all(col_send, col_recv, row_send, row_recv, 0)

    wait_load(5, 6, 7)

    def first_inner(i, _):
        r, here, mid, low, high = slices(i)
        c_low = cosb[here, :]
        c_high = cosb[pl.ds(r + 1, SUB), :]
        m_low = 0.25 * (1.0 + jnp.abs(c_low))
        m_high = 0.25 * (1.0 + jnp.abs(c_high))
        wn = wnb[:, :, mid, :]
        merid = c_high * (wn + wnb[:, :, high, :]) - c_low * (wnb[:, :, low, :] + wn)
        rhsb[:, :, here, :] = fb[:, :, here, :] - 0.5 * merid
        ct = ctb[:, :, mid, :]
        w_south = m_low * (ct + ctb[:, :, low, :])
        w_north = m_high * (ct + ctb[:, :, high, :])
        swb[:, :, here, :] = w_south
        nwb[:, :, here, :] = w_north
        v = cvb[:, :, here, :]
        dg = dgb[:, :, here, :]
        upper = jnp.concatenate((v[1:], jnp.zeros_like(v[:1])), 0)
        totb[:, :, here, :] = dg + w_south + w_north + v + upper
        p = pb[:, :, mid, :]
        applied = dg * p + vertical(p, v)
        applied += w_south * (p - pb[:, :, low, :])
        appb[:, :, here, :] = applied + w_north * (p - pb[:, :, high, :])
        return 0

    def first_outer(i, _):
        r, here, mid, low, high = slices(i)
        we = web[:, :, here, :]
        zonal = shift(we, halo(hc, levels, r, wide + levels, LANES - 1), False) - shift(
            we, halo(hc, levels, r, levels, 0), True
        )
        rhs = rhsb[:, :, here, :] - 0.5 * zonal
        rhs2b[:, :, here, :] = rhs
        cl = clb[:, :, here, :]
        w_west = 0.5 * (cl + shift(cl, halo(hc, levels, r, 2 * levels, 0), True))
        w_east = 0.5 * (cl + shift(cl, halo(hc, levels, r, wide + 2 * levels, LANES - 1), False))
        wwb[:, :, here, :] = w_west
        ewb[:, :, here, :] = w_east
        total = totb[:, :, here, :] + w_west + w_east
        p = pb[:, :, mid, :]
        applied = appb[:, :, here, :]
        applied += w_west * (p - shift(p, halo(hc, levels, r, 0, 0), True))
        applied += w_east * (p - shift(p, halo(hc, levels, r, wide, LANES - 1), False))
        fresh = p + (rhs - applied) / total
        npb[:, :, mid, :] = fresh
        pk[here, :] = packed([fresh], narrow)
        return 0

    def second_inner(i, _):
        r, here, mid, low, high = slices(i)
        p = npb[:, :, mid, :]
        applied = dgb[:, :, here, :] * p + vertical(p, cvb[:, :, here, :])
        applied += swb[:, :, here, :] * (p - npb[:, :, low, :])
        applied += nwb[:, :, here, :] * (p - npb[:, :, high, :])
        accb[:, :, here, :] = rhs2b[:, :, here, :] - applied
        return 0

    def inner_rows(step, src, fields, phase):
        loop(1, chunks - 1, step)
        for slot in (2, 3):
            wait_recv(src.at[slot - 2], slot, phase)
        unpack_rows(src, fields)
        step(0, 0)
        step(chunks - 1, 0)

    inner_rows(first_inner, row_recv, (pb, wnb, ctb), 0)
    for slot in (0, 1):
        wait_recv(col_recv.at[slot], slot, 0)
    rows_to_columns(col_recv, wide)
    loop(0, chunks, first_outer)

    columns_to_rows(col2_send, narrow)
    pack_rows((npb,), row2_send)
    sends += send_all(col2_send, col2_recv, row2_send, row2_recv, 1)

    inner_rows(second_inner, row2_recv, (npb,), 1)
    for slot in (0, 1):
        wait_recv(col2_recv.at[slot], slot, 1)
    rows_to_columns(col2_recv, narrow)
    for copy in sends:
        copy.wait_send()


def lat_id(index, count):
    return lax.rem(index, count)


def per_device(lon_n, lat_n, *fields):
    levels, rows, width = fields[0].shape
    tiles = width // LANES
    blocks = -(-rows // LANES)
    f32 = jnp.float32
    plain = pltpu.VMEM((levels, tiles, rows, LANES), f32)
    padded = pltpu.VMEM((levels, tiles, rows + 2 * SUB, LANES), f32)
    wide = -(-3 * levels // SUB) * SUB
    narrow = -(-levels // SUB) * SUB
    cols = lambda n: pltpu.VMEM((2, blocks, n, LANES), f32)
    edge = lambda n: pltpu.VMEM((2, tiles, n, LANES), f32)
    any_spec = pl.BlockSpec(memory_space=pl.ANY)
    vmem_spec = pl.BlockSpec(memory_space=pltpu.VMEM)
    strip = pltpu.VMEM((blocks * LANES, LANES), f32)
    held = pl.pallas_call(
        functools.partial(kernel, lon_n, lat_n, rows * lat_n),
        out_shape=(padded, plain, plain, plain, strip),
        in_specs=[any_spec] * 8,
        out_specs=(vmem_spec,) * 5,
        scratch_shapes=[
            padded, plain, padded, plain, plain, padded, plain, plain,
        ] + [plain] * 6 + [
            pltpu.VMEM((rows + SUB, LANES), f32), strip,
            cols(wide), cols(wide), edge(wide), edge(wide),
            cols(narrow), cols(narrow), edge(narrow), edge(narrow),
            pltpu.SemaphoreType.DMA((8, tiles)),
            pltpu.SemaphoreType.DMA((2, 4)),
            pltpu.SemaphoreType.DMA((2, 4)),
        ],
        compiler_params=pltpu.CompilerParams(
            collective_id=0, has_side_effects=True, vmem_limit_bytes=44 * 1024 * 1024
        ),
    )(*(pltpu.with_memory_space_constraint(x, pltpu.HBM) for x in fields))
    result = pltpu.HBM((levels, rows, width), f32)
    return pl.pallas_call(
        functools.partial(finish, narrow),
        out_shape=(result, result),
        in_specs=[vmem_spec] * 5,
        out_specs=(any_spec, any_spec),
        scratch_shapes=[plain, pltpu.SemaphoreType.DMA((2, 3, tiles))],
        compiler_params=pltpu.CompilerParams(vmem_limit_bytes=16 * 1024 * 1024),
    )(*(pltpu.with_memory_space_constraint(x, pltpu.VMEM) for x in held))


def solution(mesh):
    spec = P(None, "lat", "lon")
    return jax.shard_map(
        functools.partial(per_device, mesh.shape["lon"], mesh.shape["lat"]),
        mesh=mesh, in_specs=(spec,) * 8, out_specs=(spec, spec), check_vma=False,
    )
```

```python
import functools
import math

import jax
import jax.numpy as jnp
from jax import lax
from jax.experimental import pallas as pl
from jax.experimental.pallas import tpu as pltpu
from jax.sharding import PartitionSpec as P

LANES = 128
SUB = 8
MESH = pl.DeviceIdType.MESH


def loop(first, last, step):
    size = max(n for n in range(1, 6) if (last - first) % n == 0)
    lax.fori_loop(first, last, step, 0, unroll=size)


def slices(i):
    r = pl.multiple_of(i * SUB, SUB)
    return r, pl.ds(r, SUB), pl.ds(r + SUB, SUB), pl.ds(r + SUB - 1, SUB), pl.ds(r + SUB + 1, SUB)


def strip_column(hc, r, lane_from, target):
    return pltpu.roll(hc[pl.ds(r, SUB), :], (target - lane_from) % LANES, 1)


def shift(x, rim, west_side):
    tiles = x.shape[1]
    lane4 = lax.broadcasted_iota(jnp.int32, x.shape, 3)
    if west_side:
        turned = pltpu.roll(x, 1, 3)
        beside = jnp.concatenate((rim, turned[:, :-1]), 1) if tiles > 1 else rim
        return jnp.where(lane4 == 0, beside, turned)
    turned = pltpu.roll(x, LANES - 1, 3)
    beside = jnp.concatenate((turned[:, 1:], rim), 1) if tiles > 1 else rim
    return jnp.where(lane4 == LANES - 1, beside, turned)


def vertical(p, v):
    lower = jnp.concatenate((jnp.zeros_like(p[:1]), p[:-1]), 0)
    flux = v * (p - lower)
    return flux - jnp.concatenate((flux[1:], jnp.zeros_like(p[:1])), 0)


def finish(narrow, npb, accb, hc, np_out, res_out, resb, sem):
    levels, tiles, rows = accb.shape[0], accb.shape[1], accb.shape[2]
    chunks = rows // SUB
    parts = max(n for n in range(1, 4) if chunks % n == 0)
    span = rows // parts
    copies = []

    def store(n, part, src, pad, dst):
        for t in range(tiles):
            copy = pltpu.make_async_copy(
                src.at[:, t, pl.ds(part * span + pad, span), :],
                dst.at[:, pl.ds(part * span, span), pl.ds(t * LANES, LANES)],
                sem.at[n, part, t],
            )
            copy.start()
            copies.append(copy)

    lane = lax.broadcasted_iota(jnp.int32, (SUB, LANES), 1)

    def step(i, _):
        r, here, mid, low, high = slices(i)
        for k in range(levels):
            for t in range(tiles):
                acc = accb[k, t, here, :]
                if t == 0:
                    acc += jnp.where(lane == 0, strip_column(hc, r, narrow + k, 0), 0.0)
                if t == tiles - 1:
                    acc += jnp.where(lane == LANES - 1, strip_column(hc, r, k, LANES - 1), 0.0)
                resb[k, t, here, :] = acc
        return 0

    for part in range(parts):
        store(0, part, npb, SUB, np_out)
    for part in range(parts):
        loop(part * (chunks // parts), (part + 1) * (chunks // parts), step)
        store(1, part, resb, 0, res_out)
    for copy in copies:
        copy.wait()


def kernel(
    lon_n, lat_n, lat_total,
    p_in, we_in, wn_in, f_in, cl_in, ct_in, cv_in, dg_in,
    npb, accb, hc,
    pb, web, wnb, fb, clb, ctb, cvb, dgb,
    rhsb, wwb, ewb, swb, nwb, cosb,
    pk, part, fix, col_send, col_recv, row_send, row_recv,
    col2_send, col2_recv, row2_send, row2_recv,
    in_sem, send_sem, recv_sem,
):
    levels, tiles, rows = web.shape[0], web.shape[1], web.shape[2]
    blocks = pk.shape[0] // LANES
    chunks = rows // SUB
    lon = lax.axis_index("lon")
    lat = lax.axis_index("lat")
    east = (lat_id(lon + 1, lon_n), lat)
    west = (lat_id(lon + lon_n - 1, lon_n), lat)
    across = lat_id(lon + lon_n // 2, lon_n)
    at_south = jnp.int32(lat == 0)
    at_north = jnp.int32(lat == lat_n - 1)
    south = (lon + at_south * (across - lon), lat - 1 + at_south)
    north = (lon + at_north * (across - lon), lat + 1 - at_north)
    partners = (west, east, south, north)

    loads = []
    for a, (src, dst, pad) in enumerate((
        (p_in, pb, SUB), (we_in, web, 0), (cl_in, clb, 0), (wn_in, wnb, SUB),
        (ct_in, ctb, SUB), (f_in, fb, 0), (cv_in, cvb, 0), (dg_in, dgb, 0),
    )):
        group = []
        for t in range(tiles):
            copy = pltpu.make_async_copy(
                src.at[:, :, pl.ds(t * LANES, LANES)],
                dst.at[:, t, pl.ds(pad, rows), :],
                in_sem.at[a, t],
            )
            group.append(copy)
        loads.append(group)

    def start_load(*which):
        for a in which:
            for copy in loads[a]:
                copy.start()

    start_load(0, 1, 2, 3, 4)

    barrier = pltpu.get_barrier_semaphore()
    for lo, la in partners:
        pl.semaphore_signal(barrier, inc=1, device_id=(lo, la), device_id_type=MESH)

    lane = lax.broadcasted_iota(jnp.int32, (SUB, LANES), 1)

    face = lat * rows + lax.broadcasted_iota(jnp.int32, cosb.shape, 0)
    cosb[...] = jnp.cos(face.astype(jnp.float32) * (math.pi / lat_total) - math.pi / 2)

    def wait_load(*which):
        for a in which:
            for copy in loads[a]:
                copy.wait()

    def packed(fields, width):
        acc = jnp.zeros((SUB, LANES), jnp.float32)
        for f, field in enumerate(fields):
            for k in range(levels):
                n = f * levels + k
                acc = jnp.where(lane == n, pltpu.roll(field[k, tiles - 1], n + 1, 1), acc)
                acc = jnp.where(lane == width + n, pltpu.roll(field[k, 0], width + n, 1), acc)
        return acc

    def pack_first(i, _):
        r = pl.multiple_of(i * SUB, SUB)
        here = pl.ds(r, SUB)
        pk[here, :] = packed(
            [pb[:, :, pl.ds(r + SUB, SUB), :], web[:, :, here, :], clb[:, :, here, :]], wide
        )
        return 0

    def columns_to_rows(dst, width):
        for u in range(blocks):
            turned = pk[pl.ds(u * LANES, LANES), :].T
            dst[0, u] = turned[:width]
            dst[1, u] = turned[width:2 * width]

    def rows_to_columns(src, width):
        for u in range(blocks):
            both = jnp.concatenate(
                (src[0, u], src[1, u], jnp.zeros((LANES - 2 * width, LANES), jnp.float32)), 0
            )
            hc[pl.ds(u * LANES, LANES), :] = both.T

    def send(n, src, dst, target, slot, phase):
        copy = pltpu.make_async_remote_copy(
            src_ref=src, dst_ref=dst,
            send_sem=send_sem.at[phase, n], recv_sem=recv_sem.at[phase, slot],
            device_id=target, device_id_type=MESH,
        )
        copy.start()
        return copy

    def wait_recv(dst, slot, phase):
        pltpu.make_async_remote_copy(
            src_ref=dst, dst_ref=dst,
            send_sem=send_sem.at[phase, slot], recv_sem=recv_sem.at[phase, slot],
            device_id=east, device_id_type=MESH,
        ).wait_recv()

    south_slot = 1 - at_south
    north_slot = at_north

    def send_columns(cs, cr, phase):
        return (
            send(0, cs.at[0], cr.at[0], east, 0, phase),
            send(1, cs.at[1], cr.at[1], west, 1, phase),
        )

    def send_rows(rs, rr, phase):
        return (
            send(2, rs.at[0], rr.at[south_slot], south, 2 + south_slot, phase),
            send(3, rs.at[1], rr.at[north_slot], north, 2 + north_slot, phase),
        )

    def pack_rows(fields, dst):
        for f, ref in enumerate(fields):
            for k in range(levels):
                n = f * levels + k
                for t in range(tiles):
                    dst[0, t, n:n + 1, :] = ref[k, t, SUB:SUB + 1, :]
                    dst[1, t, n:n + 1, :] = ref[k, t, SUB + rows - 1:SUB + rows, :]

    def unpack_rows(src, fields):
        for f, ref in enumerate(fields):
            for k in range(levels):
                n = f * levels + k
                for t in range(tiles):
                    ref[k, t, SUB - 1:SUB, :] = src[0, t, n:n + 1, :]
                    ref[k, t, SUB + rows:SUB + rows + 1, :] = src[1, t, n:n + 1, :]

    if blocks * LANES > rows:
        pk[pl.ds(rows, blocks * LANES - rows), :] = jnp.zeros(
            (blocks * LANES - rows, LANES), jnp.float32
        )
    wide = col_send.shape[2]
    narrow = col2_send.shape[2]
    pair = part.shape[2]
    row_send[...] = jnp.zeros(row_send.shape, jnp.float32)
    row2_send[...] = jnp.zeros(row2_send.shape, jnp.float32)
    col2_send[...] = jnp.zeros(col2_send.shape, jnp.float32)
    fix[...] = jnp.zeros(fix.shape, jnp.float32)

    wait_load(0, 1, 2)
    start_load(5, 6, 7)
    loop(0, chunks, pack_first)
    columns_to_rows(col_send, wide)
    pl.semaphore_wait(barrier, len(partners))
    sends = send_columns(col_send, col_recv, 0)
    wait_load(3, 4)
    pack_rows((pb, wnb, ctb), row_send)
    sends += send_rows(row_send, row_recv, 0)

    wait_load(5, 6, 7)

    def first_pass(i, _):
        r, here, mid, low, high = slices(i)
        c_low = cosb[here, :]
        c_high = cosb[pl.ds(r + 1, SUB), :]
        m_low = 0.25 * (1.0 + jnp.abs(c_low))
        m_high = 0.25 * (1.0 + jnp.abs(c_high))
        we = web[:, :, here, :]
        none = jnp.zeros_like(we[:, :1])
        zonal = shift(we, none, False) - shift(we, none, True)
        wn = wnb[:, :, mid, :]
        merid = c_high * (wn + wnb[:, :, high, :]) - c_low * (wnb[:, :, low, :] + wn)
        rhs = fb[:, :, here, :] - 0.5 * (zonal + merid)
        rhsb[:, :, here, :] = rhs
        cl = clb[:, :, here, :]
        w_west = 0.5 * (cl + shift(cl, -cl[:, :1], True))
        w_east = 0.5 * (cl + shift(cl, -cl[:, -1:], False))
        wwb[:, :, here, :] = w_west
        ewb[:, :, here, :] = w_east
        ct = ctb[:, :, mid, :]
        w_south = m_low * (ct + ctb[:, :, low, :])
        w_north = m_high * (ct + ctb[:, :, high, :])
        swb[:, :, here, :] = w_south
        nwb[:, :, here, :] = w_north
        v = cvb[:, :, here, :]
        dg = dgb[:, :, here, :]
        upper = jnp.concatenate((v[1:], jnp.zeros_like(v[:1])), 0)
        total = dg + w_west + w_east + w_south + w_north + v + upper
        p = pb[:, :, mid, :]
        applied = dg * p + vertical(p, v)
        applied += w_west * (p - shift(p, none, True))
        applied += w_east * (p - shift(p, none, False))
        applied += w_south * (p - pb[:, :, low, :])
        applied += w_north * (p - pb[:, :, high, :])
        short = rhs - applied
        npb[:, :, mid, :] = p + short / total
        pk[here, :] = packed([short, total], pair)
        return 0

    def merge(i, _):
        r, here, mid, low, high = slices(i)
        for k in range(levels):
            npb[k, 0, mid, :] = jnp.where(
                lane == 0, strip_column(hc, r, narrow + k, 0), npb[k, 0, mid, :]
            )
            npb[k, tiles - 1, mid, :] = jnp.where(
                lane == LANES - 1, strip_column(hc, r, k, LANES - 1), npb[k, tiles - 1, mid, :]
            )
        return 0

    def second_pass(i, _):
        r, here, mid, low, high = slices(i)
        p = npb[:, :, mid, :]
        none = jnp.zeros_like(p[:, :1])
        applied = dgb[:, :, here, :] * p + vertical(p, cvb[:, :, here, :])
        applied += wwb[:, :, here, :] * (p - shift(p, none, True))
        applied += ewb[:, :, here, :] * (p - shift(p, none, False))
        applied += swb[:, :, here, :] * (p - npb[:, :, low, :])
        applied += nwb[:, :, here, :] * (p - npb[:, :, high, :])
        accb[:, :, here, :] = rhsb[:, :, here, :] - applied
        return 0

    def inner_rows(step, src, fields, phase):
        loop(1, chunks - 1, step)
        for slot in (2, 3):
            wait_recv(src.at[slot - 2], slot, phase)
        unpack_rows(src, fields)
        step(0, 0)
        step(chunks - 1, 0)

    inner_rows(first_pass, row_recv, (pb, wnb, ctb), 0)
    columns_to_rows(part, pair)
    for slot in (0, 1):
        wait_recv(col_recv.at[slot], slot, 0)

    edges = []
    for side in (0, 1):
        for u in range(blocks):
            own, other = col_send[side, u], col_recv[1 - side, u]
            p = own[:levels]
            weight = 0.5 * (own[2 * levels:3 * levels] + other[2 * levels:3 * levels])
            gain = (side - 0.5) * other[levels:2 * levels]
            short = part[side, u, :levels, :] + gain - weight * (p - other[:levels])
            total = part[side, u, levels:2 * levels, :] + weight
            fresh = p + short / jnp.where(total > 0.0, total, 1.0)
            col2_send[side, u, :levels, :] = fresh
            edges.append((side, u, weight, gain, fresh))
    sends += send_columns(col2_send, col2_recv, 1)
    rows_to_columns(col2_send, narrow)
    loop(0, chunks, merge)
    pack_rows((npb,), row2_send)
    sends += send_rows(row2_send, row2_recv, 1)

    inner_rows(second_pass, row2_recv, (npb,), 1)
    for slot in (0, 1):
        wait_recv(col2_recv.at[slot], slot, 1)
    for side, u, weight, gain, fresh in edges:
        fix[side, u, :levels, :] = gain - weight * (fresh - col2_recv[1 - side, u, :levels, :])
    rows_to_columns(fix, narrow)
    for copy in sends:
        copy.wait_send()


def lat_id(index, count):
    return lax.rem(index, count)


def per_device(lon_n, lat_n, *fields):
    levels, rows, width = fields[0].shape
    tiles = width // LANES
    blocks = -(-rows // LANES)
    f32 = jnp.float32
    plain = pltpu.VMEM((levels, tiles, rows, LANES), f32)
    padded = pltpu.VMEM((levels, tiles, rows + 2 * SUB, LANES), f32)
    wide = -(-3 * levels // SUB) * SUB
    narrow = -(-levels // SUB) * SUB
    pair = -(-2 * levels // SUB) * SUB
    cols = lambda n: pltpu.VMEM((2, blocks, n, LANES), f32)
    edge = lambda n: pltpu.VMEM((2, tiles, n, LANES), f32)
    any_spec = pl.BlockSpec(memory_space=pl.ANY)
    vmem_spec = pl.BlockSpec(memory_space=pltpu.VMEM)
    strip = pltpu.VMEM((blocks * LANES, LANES), f32)
    held = pl.pallas_call(
        functools.partial(kernel, lon_n, lat_n, rows * lat_n),
        out_shape=(padded, plain, strip),
        in_specs=[any_spec] * 8,
        out_specs=(vmem_spec,) * 3,
        scratch_shapes=[
            padded, plain, padded, plain, plain, padded, plain, plain,
        ] + [plain] * 5 + [
            pltpu.VMEM((rows + SUB, LANES), f32), strip, cols(pair), cols(narrow),
            cols(wide), cols(wide), edge(wide), edge(wide),
            cols(narrow), cols(narrow), edge(narrow), edge(narrow),
            pltpu.SemaphoreType.DMA((8, tiles)),
            pltpu.SemaphoreType.DMA((2, 4)),
            pltpu.SemaphoreType.DMA((2, 4)),
        ],
        compiler_params=pltpu.CompilerParams(
            collective_id=0, has_side_effects=True, vmem_limit_bytes=44 * 1024 * 1024
        ),
    )(*(pltpu.with_memory_space_constraint(x, pltpu.HBM) for x in fields))
    result = pltpu.HBM((levels, rows, width), f32)
    return pl.pallas_call(
        functools.partial(finish, narrow),
        out_shape=(result, result),
        in_specs=[vmem_spec] * 3,
        out_specs=(any_spec, any_spec),
        scratch_shapes=[plain, pltpu.SemaphoreType.DMA((2, 3, tiles))],
        compiler_params=pltpu.CompilerParams(vmem_limit_bytes=16 * 1024 * 1024),
    )(*(pltpu.with_memory_space_constraint(x, pltpu.VMEM) for x in held))


def solution(mesh):
    spec = P(None, "lat", "lon")
    return jax.shard_map(
        functools.partial(per_device, mesh.shape["lon"], mesh.shape["lat"]),
        mesh=mesh, in_specs=(spec,) * 8, out_specs=(spec, spec), check_vma=False,
    )
```

```python
import functools
import math

import jax
import jax.numpy as jnp
from jax import lax
from jax.experimental import pallas as pl
from jax.experimental.pallas import tpu as pltpu
from jax.sharding import PartitionSpec as P

LANES = 128
SUB = 8
MESH = pl.DeviceIdType.MESH


def loop(first, last, step):
    size = max(n for n in range(1, 6) if (last - first) % n == 0)
    lax.fori_loop(first, last, step, 0, unroll=size)


def slices(i):
    r = pl.multiple_of(i * SUB, SUB)
    return r, pl.ds(r, SUB), pl.ds(r + SUB, SUB), pl.ds(r + SUB - 1, SUB), pl.ds(r + SUB + 1, SUB)


def strip_column(hc, r, lane_from, target):
    return pltpu.roll(hc[pl.ds(r, SUB), :], (target - lane_from) % LANES, 1)


def shift(x, rim, west_side):
    tiles = x.shape[1]
    lane4 = lax.broadcasted_iota(jnp.int32, x.shape, 3)
    if west_side:
        turned = pltpu.roll(x, 1, 3)
        beside = jnp.concatenate((rim, turned[:, :-1]), 1) if tiles > 1 else rim
        return jnp.where(lane4 == 0, beside, turned)
    turned = pltpu.roll(x, LANES - 1, 3)
    beside = jnp.concatenate((turned[:, 1:], rim), 1) if tiles > 1 else rim
    return jnp.where(lane4 == LANES - 1, beside, turned)


def vertical(p, v):
    lower = jnp.concatenate((jnp.zeros_like(p[:1]), p[:-1]), 0)
    flux = v * (p - lower)
    return flux - jnp.concatenate((flux[1:], jnp.zeros_like(p[:1])), 0)


def finish(narrow, npb, accb, hc, np_out, res_out, resb, sem):
    levels, tiles, rows = accb.shape[0], accb.shape[1], accb.shape[2]
    chunks = rows // SUB
    parts = max(n for n in range(1, 4) if chunks % n == 0)
    span = rows // parts
    copies = []

    def store(n, part, src, pad, dst):
        for t in range(tiles):
            copy = pltpu.make_async_copy(
                src.at[:, t, pl.ds(part * span + pad, span), :],
                dst.at[:, pl.ds(part * span, span), pl.ds(t * LANES, LANES)],
                sem.at[n, part, t],
            )
            copy.start()
            copies.append(copy)

    lane = lax.broadcasted_iota(jnp.int32, (SUB, LANES), 1)

    def step(i, _):
        r, here, mid, low, high = slices(i)
        for k in range(levels):
            for t in range(tiles):
                acc = accb[k, t, here, :]
                if t == 0:
                    acc += jnp.where(lane == 0, strip_column(hc, r, narrow + k, 0), 0.0)
                if t == tiles - 1:
                    acc += jnp.where(lane == LANES - 1, strip_column(hc, r, k, LANES - 1), 0.0)
                resb[k, t, here, :] = acc
        return 0

    for part in range(parts):
        store(0, part, npb, SUB, np_out)
    for part in range(parts):
        loop(part * (chunks // parts), (part + 1) * (chunks // parts), step)
        store(1, part, resb, 0, res_out)
    for copy in copies:
        copy.wait()


def kernel(
    lon_n, lat_n, lat_total,
    p_in, we_in, wn_in, f_in, cl_in, ct_in, cv_in, dg_in,
    npb, accb, hc,
    pb, web, wnb, fb, clb, ctb, cvb, dgb,
    rhsb, wwb, ewb, swb, nwb, cosb,
    pk, part, fix, col_send, col_recv, row_send, row_recv,
    col2_send, col2_recv, row2_send, row2_recv,
    in_sem, send_sem, recv_sem,
):
    levels, tiles, rows = web.shape[0], web.shape[1], web.shape[2]
    blocks = pk.shape[0] // LANES
    chunks = rows // SUB
    lon = lax.axis_index("lon")
    lat = lax.axis_index("lat")
    east = (lat_id(lon + 1, lon_n), lat)
    west = (lat_id(lon + lon_n - 1, lon_n), lat)
    across = lat_id(lon + lon_n // 2, lon_n)
    at_south = jnp.int32(lat == 0)
    at_north = jnp.int32(lat == lat_n - 1)
    south = (lon + at_south * (across - lon), lat - 1 + at_south)
    north = (lon + at_north * (across - lon), lat + 1 - at_north)
    partners = (west, east, south, north)

    loads = []
    for a, (src, dst, pad) in enumerate((
        (p_in, pb, SUB), (we_in, web, 0), (cl_in, clb, 0), (wn_in, wnb, SUB),
        (ct_in, ctb, SUB), (f_in, fb, 0), (cv_in, cvb, 0), (dg_in, dgb, 0),
    )):
        group = []
        for t in range(tiles):
            copy = pltpu.make_async_copy(
                src.at[:, :, pl.ds(t * LANES, LANES)],
                dst.at[:, t, pl.ds(pad, rows), :],
                in_sem.at[a, t],
            )
            group.append(copy)
        loads.append(group)

    def start_load(*which):
        for a in which:
            for copy in loads[a]:
                copy.start()

    start_load(0, 1, 2)

    barrier = pltpu.get_barrier_semaphore()
    for lo, la in partners:
        pl.semaphore_signal(barrier, inc=1, device_id=(lo, la), device_id_type=MESH)

    lane = lax.broadcasted_iota(jnp.int32, (SUB, LANES), 1)

    face = lat * rows + lax.broadcasted_iota(jnp.int32, cosb.shape, 0)
    cosb[...] = jnp.cos(face.astype(jnp.float32) * (math.pi / lat_total) - math.pi / 2)

    def wait_load(*which):
        for a in which:
            for copy in loads[a]:
                copy.wait()

    def packed(fields, width):
        acc = jnp.zeros((SUB, LANES), jnp.float32)
        for f, field in enumerate(fields):
            for k in range(levels):
                n = f * levels + k
                acc = jnp.where(lane == n, pltpu.roll(field[k, tiles - 1], n + 1, 1), acc)
                acc = jnp.where(lane == width + n, pltpu.roll(field[k, 0], width + n, 1), acc)
        return acc

    def pack_first(i, _):
        r = pl.multiple_of(i * SUB, SUB)
        here = pl.ds(r, SUB)
        pk[here, :] = packed(
            [pb[:, :, pl.ds(r + SUB, SUB), :], web[:, :, here, :], clb[:, :, here, :]], wide
        )
        return 0

    def columns_to_rows(dst, width):
        for u in range(blocks):
            turned = pk[pl.ds(u * LANES, LANES), :].T
            dst[0, u] = turned[:width]
            dst[1, u] = turned[width:2 * width]

    def rows_to_columns(src, width):
        for u in range(blocks):
            both = jnp.concatenate(
                (src[0, u], src[1, u], jnp.zeros((LANES - 2 * width, LANES), jnp.float32)), 0
            )
            hc[pl.ds(u * LANES, LANES), :] = both.T

    def send(n, src, dst, target, slot, phase):
        copy = pltpu.make_async_remote_copy(
            src_ref=src, dst_ref=dst,
            send_sem=send_sem.at[phase, n], recv_sem=recv_sem.at[phase, slot],
            device_id=target, device_id_type=MESH,
        )
        copy.start()
        return copy

    def wait_recv(dst, slot, phase):
        pltpu.make_async_remote_copy(
            src_ref=dst, dst_ref=dst,
            send_sem=send_sem.at[phase, slot], recv_sem=recv_sem.at[phase, slot],
            device_id=east, device_id_type=MESH,
        ).wait_recv()

    south_slot = 1 - at_south
    north_slot = at_north

    def send_columns(cs, cr, phase):
        return (
            send(0, cs.at[0], cr.at[0], east, 0, phase),
            send(1, cs.at[1], cr.at[1], west, 1, phase),
        )

    def send_rows(rs, rr, phase):
        return (
            send(2, rs.at[0], rr.at[south_slot], south, 2 + south_slot, phase),
            send(3, rs.at[1], rr.at[north_slot], north, 2 + north_slot, phase),
        )

    def pack_rows(fields, dst):
        for f, ref in enumerate(fields):
            for k in range(levels):
                n = f * levels + k
                for t in range(tiles):
                    dst[0, t, n:n + 1, :] = ref[k, t, SUB:SUB + 1, :]
                    dst[1, t, n:n + 1, :] = ref[k, t, SUB + rows - 1:SUB + rows, :]

    def unpack_rows(src, fields):
        for f, ref in enumerate(fields):
            for k in range(levels):
                n = f * levels + k
                for t in range(tiles):
                    ref[k, t, SUB - 1:SUB, :] = src[0, t, n:n + 1, :]
                    ref[k, t, SUB + rows:SUB + rows + 1, :] = src[1, t, n:n + 1, :]

    if blocks * LANES > rows:
        pk[pl.ds(rows, blocks * LANES - rows), :] = jnp.zeros(
            (blocks * LANES - rows, LANES), jnp.float32
        )
    wide = col_send.shape[2]
    narrow = col2_send.shape[2]
    pair = part.shape[2]
    row_send[...] = jnp.zeros(row_send.shape, jnp.float32)
    row2_send[...] = jnp.zeros(row2_send.shape, jnp.float32)
    col2_send[...] = jnp.zeros(col2_send.shape, jnp.float32)
    fix[...] = jnp.zeros(fix.shape, jnp.float32)

    wait_load(0)
    start_load(3, 4)
    wait_load(1, 2)
    start_load(5, 6, 7)
    loop(0, chunks, pack_first)
    columns_to_rows(col_send, wide)
    pl.semaphore_wait(barrier, len(partners))
    sends = send_columns(col_send, col_recv, 0)
    wait_load(3, 4)
    pack_rows((pb, wnb, ctb), row_send)
    sends += send_rows(row_send, row_recv, 0)

    wait_load(5, 6, 7)

    def first_pass(i, _):
        r, here, mid, low, high = slices(i)
        c_low = cosb[here, :]
        c_high = cosb[pl.ds(r + 1, SUB), :]
        m_low = 0.25 * (1.0 + jnp.abs(c_low))
        m_high = 0.25 * (1.0 + jnp.abs(c_high))
        we = web[:, :, here, :]
        none = jnp.zeros_like(we[:, :1])
        zonal = shift(we, none, False) - shift(we, none, True)
        wn = wnb[:, :, mid, :]
        merid = c_high * (wn + wnb[:, :, high, :]) - c_low * (wnb[:, :, low, :] + wn)
        rhs = fb[:, :, here, :] - 0.5 * (zonal + merid)
        rhsb[:, :, here, :] = rhs
        cl = clb[:, :, here, :]
        w_west = 0.5 * (cl + shift(cl, -cl[:, :1], True))
        w_east = 0.5 * (cl + shift(cl, -cl[:, -1:], False))
        wwb[:, :, here, :] = w_west
        ewb[:, :, here, :] = w_east
        ct = ctb[:, :, mid, :]
        w_south = m_low * (ct + ctb[:, :, low, :])
        w_north = m_high * (ct + ctb[:, :, high, :])
        swb[:, :, here, :] = w_south
        nwb[:, :, here, :] = w_north
        v = cvb[:, :, here, :]
        dg = dgb[:, :, here, :]
        upper = jnp.concatenate((v[1:], jnp.zeros_like(v[:1])), 0)
        total = dg + w_west + w_east + w_south + w_north + v + upper
        p = pb[:, :, mid, :]
        applied = dg * p + vertical(p, v)
        applied += w_west * (p - shift(p, none, True))
        applied += w_east * (p - shift(p, none, False))
        applied += w_south * (p - pb[:, :, low, :])
        applied += w_north * (p - pb[:, :, high, :])
        short = rhs - applied
        npb[:, :, mid, :] = p + short / total
        pk[here, :] = packed([short, total], pair)
        return 0

    def merge(i, _):
        r, here, mid, low, high = slices(i)
        for k in range(levels):
            npb[k, 0, mid, :] = jnp.where(
                lane == 0, strip_column(hc, r, narrow + k, 0), npb[k, 0, mid, :]
            )
            npb[k, tiles - 1, mid, :] = jnp.where(
                lane == LANES - 1, strip_column(hc, r, k, LANES - 1), npb[k, tiles - 1, mid, :]
            )
        return 0

    def second_pass(i, _):
        r, here, mid, low, high = slices(i)
        p = npb[:, :, mid, :]
        none = jnp.zeros_like(p[:, :1])
        applied = dgb[:, :, here, :] * p + vertical(p, cvb[:, :, here, :])
        applied += wwb[:, :, here, :] * (p - shift(p, none, True))
        applied += ewb[:, :, here, :] * (p - shift(p, none, False))
        applied += swb[:, :, here, :] * (p - npb[:, :, low, :])
        applied += nwb[:, :, here, :] * (p - npb[:, :, high, :])
        accb[:, :, here, :] = rhsb[:, :, here, :] - applied
        return 0

    def inner_rows(step, src, fields, phase):
        loop(1, chunks - 1, step)
        for slot in (2, 3):
            wait_recv(src.at[slot - 2], slot, phase)
        unpack_rows(src, fields)
        step(0, 0)
        step(chunks - 1, 0)

    inner_rows(first_pass, row_recv, (pb, wnb, ctb), 0)
    columns_to_rows(part, pair)
    for slot in (0, 1):
        wait_recv(col_recv.at[slot], slot, 0)

    edges = []
    for side in (0, 1):
        for u in range(blocks):
            own, other = col_send[side, u], col_recv[1 - side, u]
            p = own[:levels]
            weight = 0.5 * (own[2 * levels:3 * levels] + other[2 * levels:3 * levels])
            gain = (side - 0.5) * other[levels:2 * levels]
            short = part[side, u, :levels, :] + gain - weight * (p - other[:levels])
            total = part[side, u, levels:2 * levels, :] + weight
            fresh = p + short / jnp.where(total > 0.0, total, 1.0)
            col2_send[side, u, :levels, :] = fresh
            edges.append((side, u, weight, gain, fresh))
    sends += send_columns(col2_send, col2_recv, 1)
    rows_to_columns(col2_send, narrow)
    merge(0, 0)
    merge(chunks - 1, 0)
    pack_rows((npb,), row2_send)
    sends += send_rows(row2_send, row2_recv, 1)
    loop(1, chunks - 1, merge)

    inner_rows(second_pass, row2_recv, (npb,), 1)
    for slot in (0, 1):
        wait_recv(col2_recv.at[slot], slot, 1)
    for side, u, weight, gain, fresh in edges:
        fix[side, u, :levels, :] = gain - weight * (fresh - col2_recv[1 - side, u, :levels, :])
    rows_to_columns(fix, narrow)
    for copy in sends:
        copy.wait_send()


def lat_id(index, count):
    return lax.rem(index, count)


def per_device(lon_n, lat_n, *fields):
    levels, rows, width = fields[0].shape
    tiles = width // LANES
    blocks = -(-rows // LANES)
    f32 = jnp.float32
    plain = pltpu.VMEM((levels, tiles, rows, LANES), f32)
    padded = pltpu.VMEM((levels, tiles, rows + 2 * SUB, LANES), f32)
    wide = -(-3 * levels // SUB) * SUB
    narrow = -(-levels // SUB) * SUB
    pair = -(-2 * levels // SUB) * SUB
    cols = lambda n: pltpu.VMEM((2, blocks, n, LANES), f32)
    edge = lambda n: pltpu.VMEM((2, tiles, n, LANES), f32)
    any_spec = pl.BlockSpec(memory_space=pl.ANY)
    vmem_spec = pl.BlockSpec(memory_space=pltpu.VMEM)
    strip = pltpu.VMEM((blocks * LANES, LANES), f32)
    held = pl.pallas_call(
        functools.partial(kernel, lon_n, lat_n, rows * lat_n),
        out_shape=(padded, plain, strip),
        in_specs=[any_spec] * 8,
        out_specs=(vmem_spec,) * 3,
        scratch_shapes=[
            padded, plain, padded, plain, plain, padded, plain, plain,
        ] + [plain] * 5 + [
            pltpu.VMEM((rows + SUB, LANES), f32), strip, cols(pair), cols(narrow),
            cols(wide), cols(wide), edge(wide), edge(wide),
            cols(narrow), cols(narrow), edge(narrow), edge(narrow),
            pltpu.SemaphoreType.DMA((8, tiles)),
            pltpu.SemaphoreType.DMA((2, 4)),
            pltpu.SemaphoreType.DMA((2, 4)),
        ],
        compiler_params=pltpu.CompilerParams(
            collective_id=0, has_side_effects=True, vmem_limit_bytes=44 * 1024 * 1024
        ),
    )(*(pltpu.with_memory_space_constraint(x, pltpu.HBM) for x in fields))
    result = pltpu.HBM((levels, rows, width), f32)
    return pl.pallas_call(
        functools.partial(finish, narrow),
        out_shape=(result, result),
        in_specs=[vmem_spec] * 3,
        out_specs=(any_spec, any_spec),
        scratch_shapes=[plain, pltpu.SemaphoreType.DMA((2, 3, tiles))],
        compiler_params=pltpu.CompilerParams(vmem_limit_bytes=16 * 1024 * 1024),
    )(*(pltpu.with_memory_space_constraint(x, pltpu.VMEM) for x in held))


def solution(mesh):
    spec = P(None, "lat", "lon")
    return jax.shard_map(
        functools.partial(per_device, mesh.shape["lon"], mesh.shape["lat"]),
        mesh=mesh, in_specs=(spec,) * 8, out_specs=(spec, spec), check_vma=False,
    )
```

```python
import functools
import math

import jax
import jax.numpy as jnp
from jax import lax
from jax.experimental import pallas as pl
from jax.experimental.pallas import tpu as pltpu
from jax.sharding import PartitionSpec as P

LANES = 128
SUB = 8
MESH = pl.DeviceIdType.MESH


def loop(first, last, step):
    size = max(n for n in range(1, 3) if (last - first) % n == 0)
    lax.fori_loop(first, last, step, 0, unroll=size)


def slices(i):
    r = pl.multiple_of(i * SUB, SUB)
    return r, pl.ds(r, SUB), pl.ds(r + SUB, SUB), pl.ds(r + SUB - 1, SUB), pl.ds(r + SUB + 1, SUB)


def strip_column(hc, r, lane_from, target):
    return pltpu.roll(hc[pl.ds(r, SUB), :], (target - lane_from) % LANES, 1)


def shift(x, rim, west_side):
    tiles = x.shape[1]
    lane4 = lax.broadcasted_iota(jnp.int32, x.shape, 3)
    if west_side:
        turned = pltpu.roll(x, 1, 3)
        beside = jnp.concatenate((rim, turned[:, :-1]), 1) if tiles > 1 else rim
        return jnp.where(lane4 == 0, beside, turned)
    turned = pltpu.roll(x, LANES - 1, 3)
    beside = jnp.concatenate((turned[:, 1:], rim), 1) if tiles > 1 else rim
    return jnp.where(lane4 == LANES - 1, beside, turned)


def vertical(p, v):
    lower = jnp.concatenate((jnp.zeros_like(p[:1]), p[:-1]), 0)
    flux = v * (p - lower)
    return flux - jnp.concatenate((flux[1:], jnp.zeros_like(p[:1])), 0)


def finish(narrow, npb, accb, hc, np_out, res_out, resb, sem):
    levels, tiles, rows = accb.shape[0], accb.shape[1], accb.shape[2]
    chunks = rows // SUB
    parts = max(n for n in range(1, 4) if chunks % n == 0)
    span = rows // parts
    copies = []

    def store(n, part, src, pad, dst):
        for t in range(tiles):
            copy = pltpu.make_async_copy(
                src.at[:, t, pl.ds(part * span + pad, span), :],
                dst.at[:, pl.ds(part * span, span), pl.ds(t * LANES, LANES)],
                sem.at[n, part, t],
            )
            copy.start()
            copies.append(copy)

    lane = lax.broadcasted_iota(jnp.int32, (SUB, LANES), 1)

    def step(i, _):
        r, here, mid, low, high = slices(i)
        for k in range(levels):
            for t in range(tiles):
                acc = accb[k, t, here, :]
                if t == 0:
                    acc += jnp.where(lane == 0, strip_column(hc, r, narrow + k, 0), 0.0)
                if t == tiles - 1:
                    acc += jnp.where(lane == LANES - 1, strip_column(hc, r, k, LANES - 1), 0.0)
                resb[k, t, here, :] = acc
        return 0

    for part in range(parts):
        store(0, part, npb, SUB, np_out)
    for part in range(parts):
        loop(part * (chunks // parts), (part + 1) * (chunks // parts), step)
        store(1, part, resb, 0, res_out)
    for copy in copies:
        copy.wait()


def kernel(
    lon_n, lat_n, lat_total,
    p_in, we_in, wn_in, f_in, cl_in, ct_in, cv_in, dg_in,
    npb, accb, hc,
    pb, web, wnb, fb, clb, ctb, cvb, dgb,
    rhsb, wwb, ewb, swb, nwb, cosb,
    pk, part, fix, col_send, col_recv, row_send, row_recv,
    col2_send, col2_recv, row2_send, row2_recv,
    in_sem, send_sem, recv_sem,
):
    levels, tiles, rows = web.shape[0], web.shape[1], web.shape[2]
    blocks = pk.shape[0] // LANES
    chunks = rows // SUB
    lon = lax.axis_index("lon")
    lat = lax.axis_index("lat")
    east = (lat_id(lon + 1, lon_n), lat)
    west = (lat_id(lon + lon_n - 1, lon_n), lat)
    across = lat_id(lon + lon_n // 2, lon_n)
    at_south = jnp.int32(lat == 0)
    at_north = jnp.int32(lat == lat_n - 1)
    south = (lon + at_south * (across - lon), lat - 1 + at_south)
    north = (lon + at_north * (across - lon), lat + 1 - at_north)
    partners = (west, east, south, north)

    loads = []
    for a, (src, dst, pad) in enumerate((
        (p_in, pb, SUB), (we_in, web, 0), (cl_in, clb, 0), (wn_in, wnb, SUB),
        (ct_in, ctb, SUB), (f_in, fb, 0), (cv_in, cvb, 0), (dg_in, dgb, 0),
    )):
        group = []
        for t in range(tiles):
            copy = pltpu.make_async_copy(
                src.at[:, :, pl.ds(t * LANES, LANES)],
                dst.at[:, t, pl.ds(pad, rows), :],
                in_sem.at[a, t],
            )
            group.append(copy)
        loads.append(group)

    def start_load(*which):
        for a in which:
            for copy in loads[a]:
                copy.start()

    start_load(0, 1, 2)

    barrier = pltpu.get_barrier_semaphore()
    for lo, la in partners:
        pl.semaphore_signal(barrier, inc=1, device_id=(lo, la), device_id_type=MESH)

    lane = lax.broadcasted_iota(jnp.int32, (SUB, LANES), 1)

    face = lat * rows + lax.broadcasted_iota(jnp.int32, cosb.shape, 0)
    cosb[...] = jnp.cos(face.astype(jnp.float32) * (math.pi / lat_total) - math.pi / 2)

    def wait_load(*which):
        for a in which:
            for copy in loads[a]:
                copy.wait()

    def packed(fields, width):
        acc = jnp.zeros((SUB, LANES), jnp.float32)
        for f, field in enumerate(fields):
            for k in range(levels):
                n = f * levels + k
                acc = jnp.where(lane == n, pltpu.roll(field[k, tiles - 1], n + 1, 1), acc)
                acc = jnp.where(lane == width + n, pltpu.roll(field[k, 0], width + n, 1), acc)
        return acc

    def pack_first(i, _):
        r = pl.multiple_of(i * SUB, SUB)
        here = pl.ds(r, SUB)
        pk[here, :] = packed(
            [pb[:, :, pl.ds(r + SUB, SUB), :], web[:, :, here, :], clb[:, :, here, :]], wide
        )
        return 0

    def columns_to_rows(dst, width):
        for u in range(blocks):
            turned = pk[pl.ds(u * LANES, LANES), :].T
            dst[0, u] = turned[:width]
            dst[1, u] = turned[width:2 * width]

    def rows_to_columns(src, width):
        for u in range(blocks):
            both = jnp.concatenate(
                (src[0, u], src[1, u], jnp.zeros((LANES - 2 * width, LANES), jnp.float32)), 0
            )
            hc[pl.ds(u * LANES, LANES), :] = both.T

    def send(n, src, dst, target, slot, phase):
        copy = pltpu.make_async_remote_copy(
            src_ref=src, dst_ref=dst,
            send_sem=send_sem.at[phase, n], recv_sem=recv_sem.at[phase, slot],
            device_id=target, device_id_type=MESH,
        )
        copy.start()
        return copy

    def wait_recv(dst, slot, phase):
        pltpu.make_async_remote_copy(
            src_ref=dst, dst_ref=dst,
            send_sem=send_sem.at[phase, slot], recv_sem=recv_sem.at[phase, slot],
            device_id=east, device_id_type=MESH,
        ).wait_recv()

    south_slot = 1 - at_south
    north_slot = at_north

    def send_columns(cs, cr, phase):
        return (
            send(0, cs.at[0], cr.at[0], east, 0, phase),
            send(1, cs.at[1], cr.at[1], west, 1, phase),
        )

    def send_rows(rs, rr, phase):
        return (
            send(2, rs.at[0], rr.at[south_slot], south, 2 + south_slot, phase),
            send(3, rs.at[1], rr.at[north_slot], north, 2 + north_slot, phase),
        )

    def pack_rows(fields, dst):
        for f, ref in enumerate(fields):
            for k in range(levels):
                n = f * levels + k
                for t in range(tiles):
                    dst[0, t, n:n + 1, :] = ref[k, t, SUB:SUB + 1, :]
                    dst[1, t, n:n + 1, :] = ref[k, t, SUB + rows - 1:SUB + rows, :]

    def unpack_rows(src, fields):
        for f, ref in enumerate(fields):
            for k in range(levels):
                n = f * levels + k
                for t in range(tiles):
                    ref[k, t, SUB - 1:SUB, :] = src[0, t, n:n + 1, :]
                    ref[k, t, SUB + rows:SUB + rows + 1, :] = src[1, t, n:n + 1, :]

    if blocks * LANES > rows:
        pk[pl.ds(rows, blocks * LANES - rows), :] = jnp.zeros(
            (blocks * LANES - rows, LANES), jnp.float32
        )
    wide = col_send.shape[2]
    narrow = col2_send.shape[2]
    pair = part.shape[2]
    row_send[...] = jnp.zeros(row_send.shape, jnp.float32)
    row2_send[...] = jnp.zeros(row2_send.shape, jnp.float32)
    col2_send[...] = jnp.zeros(col2_send.shape, jnp.float32)
    fix[...] = jnp.zeros(fix.shape, jnp.float32)

    wait_load(0)
    start_load(3, 4)
    wait_load(1, 2)
    start_load(5, 6, 7)
    loop(0, chunks, pack_first)
    columns_to_rows(col_send, wide)
    pl.semaphore_wait(barrier, len(partners))
    sends = send_columns(col_send, col_recv, 0)
    wait_load(3, 4)
    pack_rows((pb, wnb, ctb), row_send)
    sends += send_rows(row_send, row_recv, 0)

    wait_load(5, 6, 7)

    def first_pass(i, _):
        r, here, mid, low, high = slices(i)
        c_low = cosb[here, :]
        c_high = cosb[pl.ds(r + 1, SUB), :]
        m_low = 0.25 * (1.0 + jnp.abs(c_low))
        m_high = 0.25 * (1.0 + jnp.abs(c_high))
        we = web[:, :, here, :]
        none = jnp.zeros_like(we[:, :1])
        zonal = shift(we, none, False) - shift(we, none, True)
        wn = wnb[:, :, mid, :]
        merid = c_high * (wn + wnb[:, :, high, :]) - c_low * (wnb[:, :, low, :] + wn)
        rhs = fb[:, :, here, :] - 0.5 * (zonal + merid)
        rhsb[:, :, here, :] = rhs
        cl = clb[:, :, here, :]
        w_west = 0.5 * (cl + shift(cl, -cl[:, :1], True))
        w_east = 0.5 * (cl + shift(cl, -cl[:, -1:], False))
        wwb[:, :, here, :] = w_west
        ewb[:, :, here, :] = w_east
        ct = ctb[:, :, mid, :]
        w_south = m_low * (ct + ctb[:, :, low, :])
        w_north = m_high * (ct + ctb[:, :, high, :])
        swb[:, :, here, :] = w_south
        nwb[:, :, here, :] = w_north
        v = cvb[:, :, here, :]
        dg = dgb[:, :, here, :]
        upper = jnp.concatenate((v[1:], jnp.zeros_like(v[:1])), 0)
        total = dg + w_west + w_east + w_south + w_north + v + upper
        p = pb[:, :, mid, :]
        applied = dg * p + vertical(p, v)
        applied += w_west * (p - shift(p, none, True))
        applied += w_east * (p - shift(p, none, False))
        applied += w_south * (p - pb[:, :, low, :])
        applied += w_north * (p - pb[:, :, high, :])
        short = rhs - applied
        npb[:, :, mid, :] = p + short / total
        pk[here, :] = packed([short, total], pair)
        return 0

    def merge(i, _):
        r, here, mid, low, high = slices(i)
        for k in range(levels):
            npb[k, 0, mid, :] = jnp.where(
                lane == 0, strip_column(hc, r, narrow + k, 0), npb[k, 0, mid, :]
            )
            npb[k, tiles - 1, mid, :] = jnp.where(
                lane == LANES - 1, strip_column(hc, r, k, LANES - 1), npb[k, tiles - 1, mid, :]
            )
        return 0

    def second_pass(i, _):
        r, here, mid, low, high = slices(i)
        p = npb[:, :, mid, :]
        none = jnp.zeros_like(p[:, :1])
        applied = dgb[:, :, here, :] * p + vertical(p, cvb[:, :, here, :])
        applied += wwb[:, :, here, :] * (p - shift(p, none, True))
        applied += ewb[:, :, here, :] * (p - shift(p, none, False))
        applied += swb[:, :, here, :] * (p - npb[:, :, low, :])
        applied += nwb[:, :, here, :] * (p - npb[:, :, high, :])
        accb[:, :, here, :] = rhsb[:, :, here, :] - applied
        return 0

    def inner_rows(step, src, fields, phase):
        loop(1, chunks - 1, step)
        for slot in (2, 3):
            wait_recv(src.at[slot - 2], slot, phase)
        unpack_rows(src, fields)
        step(0, 0)
        step(chunks - 1, 0)

    inner_rows(first_pass, row_recv, (pb, wnb, ctb), 0)
    columns_to_rows(part, pair)
    for slot in (0, 1):
        wait_recv(col_recv.at[slot], slot, 0)

    edges = []
    for side in (0, 1):
        for u in range(blocks):
            own, other = col_send[side, u], col_recv[1 - side, u]
            p = own[:levels]
            weight = 0.5 * (own[2 * levels:3 * levels] + other[2 * levels:3 * levels])
            gain = (side - 0.5) * other[levels:2 * levels]
            short = part[side, u, :levels, :] + gain - weight * (p - other[:levels])
            total = part[side, u, levels:2 * levels, :] + weight
            fresh = p + short / jnp.where(total > 0.0, total, 1.0)
            col2_send[side, u, :levels, :] = fresh
            edges.append((side, u, weight, gain, fresh))
    sends += send_columns(col2_send, col2_recv, 1)
    rows_to_columns(col2_send, narrow)
    merge(0, 0)
    merge(chunks - 1, 0)
    pack_rows((npb,), row2_send)
    sends += send_rows(row2_send, row2_recv, 1)
    loop(1, chunks - 1, merge)

    inner_rows(second_pass, row2_recv, (npb,), 1)
    for slot in (0, 1):
        wait_recv(col2_recv.at[slot], slot, 1)
    for side, u, weight, gain, fresh in edges:
        fix[side, u, :levels, :] = gain - weight * (fresh - col2_recv[1 - side, u, :levels, :])
    rows_to_columns(fix, narrow)
    for copy in sends:
        copy.wait_send()


def lat_id(index, count):
    return lax.rem(index, count)


def per_device(lon_n, lat_n, *fields):
    levels, rows, width = fields[0].shape
    tiles = width // LANES
    blocks = -(-rows // LANES)
    f32 = jnp.float32
    plain = pltpu.VMEM((levels, tiles, rows, LANES), f32)
    padded = pltpu.VMEM((levels, tiles, rows + 2 * SUB, LANES), f32)
    wide = -(-3 * levels // SUB) * SUB
    narrow = -(-levels // SUB) * SUB
    pair = -(-2 * levels // SUB) * SUB
    cols = lambda n: pltpu.VMEM((2, blocks, n, LANES), f32)
    edge = lambda n: pltpu.VMEM((2, tiles, n, LANES), f32)
    any_spec = pl.BlockSpec(memory_space=pl.ANY)
    vmem_spec = pl.BlockSpec(memory_space=pltpu.VMEM)
    strip = pltpu.VMEM((blocks * LANES, LANES), f32)
    held = pl.pallas_call(
        functools.partial(kernel, lon_n, lat_n, rows * lat_n),
        out_shape=(padded, plain, strip),
        in_specs=[any_spec] * 8,
        out_specs=(vmem_spec,) * 3,
        scratch_shapes=[
            padded, plain, padded, plain, plain, padded, plain, plain,
        ] + [plain] * 5 + [
            pltpu.VMEM((rows + SUB, LANES), f32), strip, cols(pair), cols(narrow),
            cols(wide), cols(wide), edge(wide), edge(wide),
            cols(narrow), cols(narrow), edge(narrow), edge(narrow),
            pltpu.SemaphoreType.DMA((8, tiles)),
            pltpu.SemaphoreType.DMA((2, 4)),
            pltpu.SemaphoreType.DMA((2, 4)),
        ],
        compiler_params=pltpu.CompilerParams(
            collective_id=0, has_side_effects=True, vmem_limit_bytes=44 * 1024 * 1024
        ),
    )(*(pltpu.with_memory_space_constraint(x, pltpu.HBM) for x in fields))
    result = pltpu.HBM((levels, rows, width), f32)
    return pl.pallas_call(
        functools.partial(finish, narrow),
        out_shape=(result, result),
        in_specs=[vmem_spec] * 3,
        out_specs=(any_spec, any_spec),
        scratch_shapes=[plain, pltpu.SemaphoreType.DMA((2, 3, tiles))],
        compiler_params=pltpu.CompilerParams(vmem_limit_bytes=16 * 1024 * 1024),
    )(*(pltpu.with_memory_space_constraint(x, pltpu.VMEM) for x in held))


def solution(mesh):
    spec = P(None, "lat", "lon")
    return jax.shard_map(
        functools.partial(per_device, mesh.shape["lon"], mesh.shape["lat"]),
        mesh=mesh, in_specs=(spec,) * 8, out_specs=(spec, spec), check_vma=False,
    )
```
